32 devices in a mesh: grp: 2 (over y), row: 4 (over x, core), col: 4 (over z).
Axes of the slice: x: 2, y: 2, z: 4, core: 2. Of those that a mesh axis runs over, the one named last changes fastest.
Arguments:
- probes: float32 [64, 16, 256], P(('grp', 'row', 'col')), parts along dimension 0, may hold values from -48 to 48, as said below
- mass: float32 [64, 256], P(('grp', 'row', 'col')), parts along dimension 0, may hold values from 1.05 to 2.5
- blocks: bfloat16 [8, 4, 14, 256, 256], P(('grp', 'row'), 'col'), parts along dimension 0, may hold values from -0.00029945374 to 0
- slot_rows: int32 [8, 4, 14], P(('grp', 'row'), 'col'), parts along dimension 0, may hold values from 0 to 7, as said below
- slot_cols: int32 [8, 4, 14], P(('grp', 'row'), 'col'), parts along dimension 0, may hold values from 0 to 7, as said below
- slot_count: int32 [8, 4], P(('grp', 'row'), 'col'), parts along dimension 0, may hold values from 1 to 14, as said below
Outputs:
- solution_field: float32 [64, 16, 256], P(('grp', 'row', 'col')), parts along dimension 0
- residual: float32 [64, 16, 256], P(('grp', 'row', 'col')), parts along dimension 0
The draws below stay inside these ranges and needn't reach their ends.
There are 2 independent parts, one for each index of `grp`. The reference program is written for one: setup_inputs(seed, part) draws one part's arguments, and reference() takes and returns one part's arrays. A program takes and returns all parts, laid end to end along the dimension named above; each array names one. Nothing has to cross between parts.
Inputs may be any that keep to these rules, and one draw needn't show every extreme that they name: `probes`: probes are finite. `slot_rows`: block pairs follow a banded lattice pattern with block offsets 0, 1, 2, 3, 4, 5 and 8; every diagonal block is stored; other blocks of the band may be missing. Padding slots hold 0. `slot_cols`: padding slots hold 0. `slot_count`: some device has all 14 slots live.
All inputs are finite; a program needn't handle non-finite values.
Results may differ from the reference program's by a relative error of at most 0.0003.
Values may be sent and summed in bfloat16 or wider, within the bound.
A program may use at most 64 MiB of HBM per device.

```python
import math
import jax
import jax.numpy as jnp
from jax import lax

BLK = 256
PROBES = 16
VB_DEV = 2
ITERS = 2
NB = 32
MAXB = 14
N_ROW = 4
N_COL = 4


def pattern_tables(key):
    k_keep, k_row, k_col = jax.random.split(key, 3)
    nbr = VB_DEV * N_COL
    total_blocks = VB_DEV * N_ROW * N_COL
    plane = total_blocks // 8
    offsets = jnp.array([0, 1, 2, plane - 1, plane, plane + 1, 2 * plane], dtype=jnp.int32)
    rows = jnp.arange(N_ROW, dtype=jnp.int32)[:, None, None, None]
    cols = jnp.arange(N_COL, dtype=jnp.int32)[None, :, None, None]
    offs = offsets[None, None, :, None]
    local = jnp.arange(nbr, dtype=jnp.int32)[None, None, None, :]
    first = rows * nbr + local
    second = first + offs
    hit = (second < total_blocks) & (second // VB_DEV % N_COL == cols)
    kept = jax.random.randint(k_keep, (N_ROW, N_COL, 7, nbr), 0, 4) > 0
    full_row = jax.random.randint(k_row, (), 0, 3 * N_ROW // 4)
    full_col = jax.random.randint(k_col, (), 0, N_COL)
    forced = (rows == full_row) & (cols == full_col) | (offs == 0)
    valid = hit & (kept | forced)
    shape = (N_ROW, N_COL, 7 * nbr)
    valid_flat = valid.reshape(shape)
    local_flat = jnp.broadcast_to(local, valid.shape).reshape(shape)
    col_local = second // (VB_DEV * N_COL) * VB_DEV + second % VB_DEV
    col_flat = jnp.broadcast_to(col_local, valid.shape).reshape(shape)
    order = jnp.argsort(1 - valid_flat.astype(jnp.int32), axis=-1, stable=True)[:, :, :7 * VB_DEV]
    picked = jnp.take_along_axis(valid_flat, order, axis=-1)
    slot_rows = jnp.where(picked, jnp.take_along_axis(local_flat, order, axis=-1), 0).astype(jnp.int32)
    slot_cols = jnp.where(picked, jnp.take_along_axis(col_flat, order, axis=-1), 0).astype(jnp.int32)
    counts = jnp.sum(valid_flat.astype(jnp.int32), axis=-1).astype(jnp.int32)
    return (slot_rows, slot_cols, counts)


def draw_slot_rows(key, part):
    return pattern_tables(key)[0]


def draw_slot_cols(key, part):
    return pattern_tables(key)[1]


def draw_slot_count(key, part):
    return pattern_tables(key)[2]


def draw_probes(key, part):
    key = jax.random.fold_in(key, 11)
    k_base, k_cols = jax.random.split(key, 2)
    total_blocks = VB_DEV * N_ROW * N_COL
    position = jnp.arange(total_blocks, dtype=jnp.float32) / total_blocks
    row_scale = jnp.power(10.0, position - 0.5)[:, None, None]
    col_scale = jnp.exp(jax.random.uniform(k_cols, (1, PROBES, 1), jnp.float32, math.log(0.3), math.log(3.0)))
    values = jnp.clip(jax.random.normal(k_base, (total_blocks, PROBES, BLK), jnp.float32), -5.0, 5.0)
    return (values * row_scale * col_scale).astype(jnp.float32)


def shard_levels(rng, dims, shards, least, high):
    factor_of = 1.0
    for axis_at, shards_of in shards:
        heights = jax.random.uniform(jax.random.fold_in(jax.random.fold_in(rng, 6), axis_at), (shards_of,), jnp.float32, least / len(shards), high / len(shards))
        factor_of = factor_of * jnp.repeat(jnp.exp(heights), dims[axis_at] // shards_of).reshape((-1,) + (1,) * (len(dims) - 1 - axis_at))
    return factor_of


def setup_inputs(seed: int = 0, part: int = 0) -> dict:
    key_list = jax.random.split(jax.random.key(seed), 7)
    own_keys = jax.random.split(jax.random.fold_in(key_list[6], part), 7)
    probes = draw_probes(jax.random.fold_in(jax.random.fold_in(key_list[6], part), 71), part)
    mass = jnp.clip(1.05 + 1.45 * jax.random.uniform(own_keys[1], (NB, BLK), jnp.float32) ** shard_levels(own_keys[1], (NB, BLK), ((0, 16),), -0.2, 0.2), 1.05, 2.5)
    blocks = jnp.clip(-0.00029945374 + 0.00029945374 * jax.random.uniform(own_keys[2], (N_ROW, N_COL, MAXB, BLK, BLK), jnp.float32) ** shard_levels(own_keys[2], (N_ROW, N_COL, MAXB, BLK, BLK), ((0, 4), (1, 4)), -0.2, 0.2), -0.00029945374, 0.0).astype(jnp.bfloat16)
    slot_rows = draw_slot_rows(jax.random.fold_in(jax.random.fold_in(key_list[6], part), 71), part)
    slot_cols = draw_slot_cols(jax.random.fold_in(jax.random.fold_in(key_list[6], part), 71), part)
    slot_count = draw_slot_count(jax.random.fold_in(jax.random.fold_in(key_list[6], part), 71), part)
    return {"probes": probes, "mass": mass, "blocks": blocks, "slot_rows": slot_rows, "slot_cols": slot_cols, "slot_count": slot_count}


def gram(first, second):
    return jnp.einsum('ipk,iqk->pq', first, second, precision=lax.Precision.HIGHEST)

def solve_sym(matrix, right):
    sym = 0.5 * (matrix + matrix.T)
    factor = jnp.linalg.cholesky(sym)
    inner = lax.linalg.triangular_solve(factor, right, left_side=True, lower=True)
    return lax.linalg.triangular_solve(factor, inner, left_side=True, lower=True, transpose_a=True)

def mix(field, coef):
    return jnp.einsum('ipk,pq->iqk', field, coef, precision=lax.Precision.HIGHEST)

def apply_operator(vec, mass, blocks, slot_rows, slot_cols, slot_count):
    nbr = VB_DEV * N_COL
    slots = blocks.shape[2]
    width = blocks.shape[3]
    low = lax.optimization_barrier(vec.astype(jnp.bfloat16)).astype(jnp.float32)
    flat_blocks = blocks.reshape(N_ROW * N_COL, slots, width, width)
    flat_rows = slot_rows.reshape(N_ROW * N_COL, slots).astype(jnp.int32)
    flat_cols = slot_cols.reshape(N_ROW * N_COL, slots).astype(jnp.int32)
    flat_count = slot_count.reshape(N_ROW * N_COL).astype(jnp.int32)
    upper = (jnp.arange(width)[:, None] < jnp.arange(width)[None, :]).astype(jnp.float32)
    device_ids = jnp.arange(N_ROW * N_COL, dtype=jnp.int32)

    def step(acc, item):
        tiles, lrows, lcols, count, device = item
        row_at = device // N_COL
        col_at = device % N_COL
        grow = row_at * nbr + lrows
        gcol = (lcols // VB_DEV * N_COL + col_at) * VB_DEV + lcols % VB_DEV
        live = (jnp.arange(slots, dtype=jnp.int32) < count).astype(jnp.float32)
        on_diag = (grow == gcol)[:, None, None]
        keep = jnp.where(on_diag, upper[None, :, :], jnp.ones_like(upper)[None, :, :])
        eff = tiles.astype(jnp.float32) * keep * live[:, None, None]
        forward = jnp.einsum('spk,sjk->spj', low[gcol], eff, precision=lax.Precision.HIGHEST)
        backward = jnp.einsum('spj,sjk->spk', low[grow], eff, precision=lax.Precision.HIGHEST)
        acc = acc.at[grow].add(forward)
        acc = acc.at[gcol].add(backward)
        return (acc, None)
    start = jnp.zeros(vec.shape, jnp.float32)
    total, _ = lax.scan(step, start, (flat_blocks, flat_rows, flat_cols, flat_count, device_ids))
    return total + mass[:, None, :] * vec

def reference(probes, mass, blocks, slot_rows, slot_cols, slot_count):
    solution_field = jnp.zeros_like(probes)
    residual = probes
    direction = probes
    norm_now = gram(residual, residual)
    for step in range(ITERS):
        image = apply_operator(direction, mass, blocks, slot_rows, slot_cols, slot_count)
        alpha = solve_sym(gram(direction, image), norm_now)
        solution_field = solution_field + mix(direction, alpha)
        residual = residual - mix(image, alpha)
        if step + 1 < ITERS:
            norm_next = gram(residual, residual)
            beta = solve_sym(norm_now, norm_next)
            direction = residual + mix(direction, beta)
            norm_now = norm_next
    return (solution_field, residual)
```

```python
import functools
import jax
import jax.numpy as jnp
from jax import lax
from jax.experimental import pallas as pl
from jax.experimental.pallas import tpu as pltpu
from jax.sharding import PartitionSpec as P

MESH = pl.DeviceIdType.MESH
HIGHEST = lax.Precision.HIGHEST
SEND = jnp.float32


def matmul(a, b, a_dim, b_dim, precision=None):
    return lax.dot_general(
        a,
        b,
        (((a_dim,), (b_dim,)), ((), ())),
        precision=precision,
        preferred_element_type=jnp.float32,
    )


def repeat(count, body):
    if count <= 16:
        for k in range(count):
            body(k)
    else:
        lax.fori_loop(0, count, lambda k, c: (body(k), c)[1], 0)


def eliminate(systems):
    size = systems[0][0].shape[0]
    rows = lax.broadcasted_iota(jnp.int32, (size, 1), 0)
    for k in range(size):
        after = []
        for left, right in systems:
            left_k = left[k : k + 1, :]
            right_k = right[k : k + 1, :]
            inverse = 1.0 / left[k : k + 1, k : k + 1]
            left_k = left_k * inverse
            right_k = right_k * inverse
            factor = left[:, k : k + 1]
            here = rows == k
            after.append(
                (
                    jnp.where(here, left_k, left - factor * left_k),
                    jnp.where(here, right_k, right - factor * right_k),
                )
            )
        systems = after
    return [right for _, right in systems]


def kernel(
    n_row,
    n_col,
    dists,
    probes_hbm,
    mass_hbm,
    blocks_hbm,
    rows_ref,
    cols_ref,
    count_ref,
    solution_ref,
    residual_ref,
    field,
    mass,
    tiles,
    row_field,
    col_field,
    products,
    row_sum,
    row_send,
    col_send,
    row_recv,
    col_recv,
    image,
    gram_send,
    gram_recv,
    in_sem,
    a_send_sem,
    a_recv_sem,
    b_send_sem,
    b_recv_sem,
    g_send_sem,
    g_recv_sem,
):
    row_at = lax.axis_index("row")
    col_at = lax.axis_index("col")
    vb, width, nodes = field.shape
    slots = tiles.shape[0]
    nbr = vb * n_col
    peers = n_row * n_col - 1
    me = row_at * n_col + col_at

    def peer_of(k):
        at = lax.rem(me + k + 1, n_row * n_col)
        return {"row": at // n_col, "col": lax.rem(at, n_col)}

    def col_peer(k):
        return lax.rem(col_at + k, n_col)

    def row_peer(d):
        return lax.rem(row_at + d, n_row)

    loads = [
        pltpu.make_async_copy(probes_hbm, field, in_sem.at[0]),
        pltpu.make_async_copy(mass_hbm, mass, in_sem.at[1]),
    ]
    for s in range(slots):
        loads.append(pltpu.make_async_copy(blocks_hbm.at[0, 0, s], tiles.at[s], in_sem.at[2 + s]))
    for load in loads:
        load.start()

    barrier = pltpu.get_barrier_semaphore()

    def greet(k):
        pl.semaphore_signal(barrier, inc=1, device_id=peer_of(k), device_id_type=MESH)

    repeat(peers, greet)

    live_count = count_ref[0, 0]
    limits, row_of, col_of, row_at_index, col_at_index = [], [], [], [], []
    for s in range(slots):
        live = s < live_count
        lrow = jnp.where(live, rows_ref[0, 0, s], 0)
        lcol = jnp.where(live, cols_ref[0, 0, s], row_at * vb)
        dist = lcol // vb - row_at
        place = jnp.int32(0)
        for at, d in enumerate(dists):
            place = place + jnp.where(dist == d, at, 0)
        part = lax.rem(lcol, vb)
        grow = row_at * nbr + lrow
        gcol = (lcol // vb * n_col + col_at) * vb + part
        limits.append(jnp.where(live, jnp.where(grow == gcol, 0, -nodes), nodes))
        row_of.append(lrow)
        col_of.append(place * vb + part)
        col_at_index.append(place * vb + part)
        row_at_index.append(
            lax.rem(col_at - lrow // vb + n_col, n_col) * vb + lax.rem(lrow, vb)
        )

    def field_to_rows(step):
        to_rows = []
        for at in range(1, len(dists)):
            to_rows.append(
                pltpu.make_async_remote_copy(
                    src_ref=col_field[step].at[pl.ds(0, vb)],
                    dst_ref=col_field[step].at[pl.ds(at * vb, vb)],
                    send_sem=a_send_sem.at[step, at - 1],
                    recv_sem=a_recv_sem.at[step, at - 1],
                    device_id={"row": row_peer(n_row - dists[at]), "col": col_at},
                    device_id_type=MESH,
                )
            )
        return to_rows

    def field_to_cols(step):
        to_cols = []
        for k in range(1, n_col):
            sem = len(dists) - 2 + k
            to_cols.append(
                pltpu.make_async_remote_copy(
                    src_ref=row_field[step].at[pl.ds(0, vb)],
                    dst_ref=row_field[step].at[pl.ds(k * vb, vb)],
                    send_sem=a_send_sem.at[step, sem],
                    recv_sem=a_recv_sem.at[step, sem],
                    device_id={"row": row_at, "col": col_peer(k)},
                    device_id_type=MESH,
                )
            )
        return to_cols

    def parts_to_cols(step):
        to_cols = []
        for k in range(1, n_col):
            to_cols.append(
                pltpu.make_async_remote_copy(
                    src_ref=row_send[step].at[pl.ds(col_peer(k) * vb, vb)],
                    dst_ref=row_recv[step].at[k - 1],
                    send_sem=b_send_sem.at[step, k - 1],
                    recv_sem=b_recv_sem.at[step, k - 1],
                    device_id={"row": row_at, "col": col_peer(k)},
                    device_id_type=MESH,
                )
            )
        return to_cols

    def parts_to_rows(step):
        to_rows = []
        for at in range(1, len(dists)):
            sem = n_col - 2 + at
            to_rows.append(
                pltpu.make_async_remote_copy(
                    src_ref=col_send[step].at[at - 1],
                    dst_ref=col_recv[step].at[at - 1],
                    send_sem=b_send_sem.at[step, sem],
                    recv_sem=b_recv_sem.at[step, sem],
                    device_id={"row": row_peer(dists[at]), "col": col_at},
                    device_id_type=MESH,
                )
            )
        return to_rows

    def gram_copy(step, k):
        return pltpu.make_async_remote_copy(
            src_ref=gram_send[step],
            dst_ref=gram_recv[step].at[k],
            send_sem=g_send_sem.at[step, k],
            recv_sem=g_recv_sem.at[step, k],
            device_id=peer_of(k),
            device_id_type=MESH,
        )

    def publish(step, low):
        row_field[step][0:vb] = low
        col_field[step][0:vb] = low

    def start(copies):
        for copy in copies:
            copy.start()

    def scattered(targets, of):
        sums = []
        for target in range(targets):
            total = jnp.zeros((width, nodes), jnp.float32)
            for s in range(slots):
                total = total + jnp.where(of[s] == target, products[s], 0.0)
            sums.append(total)
        return sums

    def forward(step):
        for copy in field_to_rows(step):
            copy.wait_recv()
        for s in range(slots):
            products[s] = matmul(col_field[step][col_at_index[s]], tiles[s], 1, 1)
        for target, total in enumerate(scattered(nbr, row_of)):
            row_sum[target] = total
            row_send[step][target] = total.astype(SEND)
        start(parts_to_cols(step))

    def backward(step):
        for copy in field_to_cols(step):
            copy.wait_recv()
        for s in range(slots):
            products[s] = matmul(row_field[step][row_at_index[s]], tiles[s], 1, 0)
        sums = scattered(len(dists) * vb, col_of)
        for at in range(1, len(dists)):
            for v in range(vb):
                col_send[step][at - 1, v] = sums[at * vb + v].astype(SEND)
        start(parts_to_rows(step))
        return [sums[v] + row_sum[col_at * vb + v] for v in range(vb)]

    def combined(step, totals):
        for copy in parts_to_cols(step) + parts_to_rows(step):
            copy.wait_recv()
        for k in range(n_col - 1):
            totals = [totals[v] + row_recv[step][k, v].astype(jnp.float32) for v in range(vb)]
        for at in range(len(dists) - 1):
            totals = [totals[v] + col_recv[step][at, v].astype(jnp.float32) for v in range(vb)]
        return totals

    loads[0].wait()
    publish(0, field[...].astype(jnp.bfloat16))
    pl.semaphore_wait(barrier, peers)
    start(field_to_rows(0) + field_to_cols(0))
    ahead = lax.broadcasted_iota(jnp.int32, (nodes, nodes), 1) - lax.broadcasted_iota(
        jnp.int32, (nodes, nodes), 0
    )
    loads[1].wait()
    for s in range(slots):
        loads[2 + s].wait()
        tiles[s] = jnp.where(ahead > limits[s], tiles[s], jnp.zeros_like(tiles[s]))
    forward(0)
    totals = combined(0, backward(0))
    for v in range(vb):
        image[v] = totals[v] + mass[v : v + 1, :] * field[v]

    publish(1, image[...].astype(jnp.bfloat16))
    start(field_to_rows(1) + field_to_cols(1))

    def gram(first, second):
        total = None
        for v in range(vb):
            term = matmul(first[v], second[v], 1, 1, HIGHEST)
            total = term if total is None else total + term
        return total

    gram_send[0][:, 0:width] = gram(field, field)
    gram_send[0][:, width : 2 * width] = gram(field, image)
    gram_send[0][:, 2 * width : 3 * width] = gram(image, field)
    gram_send[0][:, 3 * width : 4 * width] = gram(image, image)
    repeat(peers, lambda k: gram_copy(0, k).start())
    forward(1)
    totals = backward(1)

    def gathered(step):
        repeat(peers, lambda k: gram_copy(step, k).wait_recv())
        total = gram_send[step][...]
        if peers <= 16:
            for k in range(peers):
                total = total + gram_recv[step][k]
            return total
        return lax.fori_loop(0, peers, lambda k, t: t + gram_recv[step][k], total)

    grams = gathered(0)
    norm = grams[:, 0:width]
    curv = grams[:, width : 2 * width]
    curv_t = grams[:, 2 * width : 3 * width]
    square = grams[:, 3 * width : 4 * width]
    unit = (
        lax.broadcasted_iota(jnp.int32, (width, width), 0)
        == lax.broadcasted_iota(jnp.int32, (width, width), 1)
    ).astype(jnp.float32)
    alpha, norm_inverse = eliminate([(0.5 * (curv + curv_t), norm), (norm, unit)])
    norm_next = (
        norm
        - matmul(curv, alpha, 1, 0, HIGHEST)
        - matmul(alpha, curv_t - matmul(square, alpha, 1, 0, HIGHEST), 0, 0, HIGHEST)
    )
    beta = matmul(norm_inverse, norm_next, 1, 0, HIGHEST)
    ahead_mix = unit + beta

    def mix(values, coef):
        return [matmul(coef, values[v], 0, 0, HIGHEST) for v in range(vb)]

    image_alpha = mix(image, alpha)
    field_alpha = mix(field, alpha)
    field_ahead = mix(field, ahead_mix)
    image_ahead = mix(image, ahead_mix)
    direction = [field_ahead[v] - image_alpha[v] for v in range(vb)]
    totals = combined(1, totals)
    second = [totals[v] + mass[v : v + 1, :] * image[v] for v in range(vb)]
    second_alpha = mix(second, alpha)
    image_next = [image_ahead[v] - second_alpha[v] for v in range(vb)]
    gram_send[1][:, 0:width] = 0.5 * (gram(direction, image_next) + gram(image_next, direction))
    repeat(peers, lambda k: gram_copy(1, k).start())
    last = gathered(1)[:, 0:width]
    (alpha_next,) = eliminate([(last, norm_next)])
    direction_alpha = mix(direction, alpha_next)
    image_next_alpha = mix(image_next, alpha_next)
    for v in range(vb):
        solution_ref[v] = field_alpha[v] + direction_alpha[v]
        residual_ref[v] = (field[v] - image_alpha[v]) - image_next_alpha[v]

    for step in range(2):
        for copies in (field_to_rows, field_to_cols, parts_to_cols, parts_to_rows):
            for copy in copies(step):
                copy.wait_send()
        repeat(peers, lambda k: gram_copy(step, k).wait_send())


def shards(probes, mass, blocks, slot_rows, slot_cols, slot_count):
    vb, width, nodes = probes.shape
    n_col = lax.axis_size("col")
    n_row = lax.axis_size("row")
    slots = blocks.shape[2]
    nbr = vb * n_col
    total_blocks = vb * n_col * n_row
    plane = total_blocks // 8
    offsets = [0, 1, 2, plane - 1, plane, plane + 1, 2 * plane]
    deltas = sorted(set([o // vb for o in offsets] + [(o + vb - 1) // vb for o in offsets]))
    dists = sorted(
        set(
            (first + d) // n_col
            for first in range(n_col)
            for d in deltas
            if (first + d) // n_col < n_row
        )
    )
    peers = n_row * n_col - 1
    low = jnp.bfloat16
    f32 = jnp.float32

    def twice(shape, dtype):
        return [pltpu.VMEM(shape, dtype), pltpu.VMEM(shape, dtype)]

    links = len(dists) - 1 + n_col - 1
    smem = pl.BlockSpec(memory_space=pltpu.SMEM)
    hbm = pl.BlockSpec(memory_space=pl.ANY)
    vmem = pl.BlockSpec(memory_space=pltpu.VMEM)
    out = jax.ShapeDtypeStruct((vb, width, nodes), f32)
    return pl.pallas_call(
        functools.partial(kernel, n_row, n_col, dists),
        out_shape=(out, out),
        in_specs=[hbm, hbm, hbm, smem, smem, smem],
        out_specs=(vmem, vmem),
        scratch_shapes=[
            pltpu.VMEM((vb, width, nodes), f32),
            pltpu.VMEM((vb, nodes), f32),
            pltpu.VMEM((slots, nodes, nodes), low),
            twice((nbr, width, nodes), low),
            twice((len(dists) * vb, width, nodes), low),
            pltpu.VMEM((slots, width, nodes), f32),
            pltpu.VMEM((nbr, width, nodes), f32),
            twice((nbr, width, nodes), SEND),
            twice((len(dists) - 1, vb, width, nodes), SEND),
            twice((n_col - 1, vb, width, nodes), SEND),
            twice((len(dists) - 1, vb, width, nodes), SEND),
            pltpu.VMEM((vb, width, nodes), f32),
            twice((width, 128), f32),
            twice((peers, width, 128), f32),
            pltpu.SemaphoreType.DMA((2 + slots,)),
            pltpu.SemaphoreType.DMA((2, links)),
            pltpu.SemaphoreType.DMA((2, links)),
            pltpu.SemaphoreType.DMA((2, links)),
            pltpu.SemaphoreType.DMA((2, links)),
            pltpu.SemaphoreType.DMA((2, peers)),
            pltpu.SemaphoreType.DMA((2, peers)),
        ],
        compiler_params=pltpu.CompilerParams(
            collective_id=0, has_side_effects=True, vmem_limit_bytes=60 * 1024 * 1024
        ),
    )(probes, mass, blocks, slot_rows, slot_cols, slot_count)


def solution(mesh):
    placed = (
        P(("grp", "row", "col"), None, None),
        P(("grp", "row", "col"), None),
        P(("grp", "row"), "col", None, None, None),
        P(("grp", "row"), "col", None),
        P(("grp", "row"), "col", None),
        P(("grp", "row"), "col"),
    )
    return jax.shard_map(
        shards,
        mesh=mesh,
        in_specs=placed,
        out_specs=(P(("grp", "row", "col"), None, None), P(("grp", "row", "col"), None, None)),
        check_vma=False,
    )
```

```python
import functools
import jax
import jax.numpy as jnp
from jax import lax
from jax.experimental import pallas as pl
from jax.experimental.pallas import tpu as pltpu
from jax.sharding import PartitionSpec as P

MESH = pl.DeviceIdType.MESH
HIGHEST = lax.Precision.HIGHEST
SEND = jnp.bfloat16


def matmul(a, b, a_dim, b_dim, precision=None):
    return lax.dot_general(
        a,
        b,
        (((a_dim,), (b_dim,)), ((), ())),
        precision=precision,
        preferred_element_type=jnp.float32,
    )


def repeat(count, body):
    if count <= 16:
        for k in range(count):
            body(k)
    else:
        lax.fori_loop(0, count, lambda k, c: (body(k), c)[1], 0)


def eliminate(systems):
    size = systems[0][0].shape[0]
    rows = lax.broadcasted_iota(jnp.int32, (size, 1), 0)
    for k in range(size):
        after = []
        for left, right in systems:
            left_k = left[k : k + 1, :]
            right_k = right[k : k + 1, :]
            inverse = 1.0 / left[k : k + 1, k : k + 1]
            left_k = left_k * inverse
            right_k = right_k * inverse
            factor = left[:, k : k + 1]
            here = rows == k
            after.append(
                (
                    jnp.where(here, left_k, left - factor * left_k),
                    jnp.where(here, right_k, right - factor * right_k),
                )
            )
        systems = after
    return [right for _, right in systems]


def kernel(
    n_row,
    n_col,
    dists,
    probes_hbm,
    mass_hbm,
    blocks_hbm,
    rows_ref,
    cols_ref,
    count_ref,
    solution_ref,
    residual_ref,
    field,
    mass,
    tiles,
    row_field,
    col_field,
    products,
    row_sum,
    row_send,
    col_send,
    row_recv,
    col_recv,
    image,
    gram_send,
    gram_recv,
    in_sem,
    a_send_sem,
    a_recv_sem,
    b_send_sem,
    b_recv_sem,
    g_send_sem,
    g_recv_sem,
):
    row_at = lax.axis_index("row")
    col_at = lax.axis_index("col")
    vb, width, nodes = field.shape
    slots = tiles.shape[0]
    nbr = vb * n_col
    peers = n_row * n_col - 1
    me = row_at * n_col + col_at

    def peer_of(k):
        at = lax.rem(me + k + 1, n_row * n_col)
        return {"row": at // n_col, "col": lax.rem(at, n_col)}

    def col_peer(k):
        return lax.rem(col_at + k, n_col)

    def row_peer(d):
        return lax.rem(row_at + d, n_row)

    loads = [
        pltpu.make_async_copy(probes_hbm, field, in_sem.at[0]),
        pltpu.make_async_copy(mass_hbm, mass, in_sem.at[1]),
    ]
    for s in range(slots):
        loads.append(pltpu.make_async_copy(blocks_hbm.at[0, 0, s], tiles.at[s], in_sem.at[2 + s]))
    for load in loads:
        load.start()

    barrier = pltpu.get_barrier_semaphore()

    def greet(k):
        pl.semaphore_signal(barrier, inc=1, device_id=peer_of(k), device_id_type=MESH)

    repeat(peers, greet)

    live_count = count_ref[0, 0]
    limits, row_of, col_of, row_at_index, col_at_index = [], [], [], [], []
    for s in range(slots):
        live = s < live_count
        lrow = jnp.where(live, rows_ref[0, 0, s], 0)
        lcol = jnp.where(live, cols_ref[0, 0, s], row_at * vb)
        dist = lcol // vb - row_at
        place = jnp.int32(0)
        for at, d in enumerate(dists):
            place = place + jnp.where(dist == d, at, 0)
        part = lax.rem(lcol, vb)
        grow = row_at * nbr + lrow
        gcol = (lcol // vb * n_col + col_at) * vb + part
        limits.append(jnp.where(live, jnp.where(grow == gcol, 0, -nodes), nodes))
        row_of.append(lrow)
        col_of.append(place * vb + part)
        col_at_index.append(place * vb + part)
        row_at_index.append(
            lax.rem(col_at - lrow // vb + n_col, n_col) * vb + lax.rem(lrow, vb)
        )

    def field_to_rows(step):
        to_rows = {}
        for at in range(1, len(dists)):
            to_rows["fr", step, at] = pltpu.make_async_remote_copy(
                src_ref=col_field[step].at[pl.ds(0, vb)],
                dst_ref=col_field[step].at[pl.ds(at * vb, vb)],
                send_sem=a_send_sem.at[step, at - 1],
                recv_sem=a_recv_sem.at[step, at - 1],
                device_id={"row": row_peer(n_row - dists[at]), "col": col_at},
                device_id_type=MESH,
            )
        return to_rows

    def field_to_cols(step):
        to_cols = {}
        for k in range(1, n_col):
            sem = len(dists) - 2 + k
            to_cols["fc", step, k] = pltpu.make_async_remote_copy(
                src_ref=row_field[step].at[pl.ds(0, vb)],
                dst_ref=row_field[step].at[pl.ds(k * vb, vb)],
                send_sem=a_send_sem.at[step, sem],
                recv_sem=a_recv_sem.at[step, sem],
                device_id={"row": row_at, "col": col_peer(k)},
                device_id_type=MESH,
            )
        return to_cols

    def parts_to_cols(step):
        to_cols = {}
        for k in range(1, n_col):
            to_cols["pc", step, k] = pltpu.make_async_remote_copy(
                src_ref=row_send[step].at[pl.ds(col_peer(k) * vb, vb)],
                dst_ref=row_recv[step].at[k - 1],
                send_sem=b_send_sem.at[step, k - 1],
                recv_sem=b_recv_sem.at[step, k - 1],
                device_id={"row": row_at, "col": col_peer(k)},
                device_id_type=MESH,
            )
        return to_cols

    def parts_to_rows(step):
        to_rows = {}
        for at in range(1, len(dists)):
            sem = n_col - 2 + at
            to_rows["pr", step, at] = pltpu.make_async_remote_copy(
                src_ref=col_send[step].at[at - 1],
                dst_ref=col_recv[step].at[at - 1],
                send_sem=b_send_sem.at[step, sem],
                recv_sem=b_recv_sem.at[step, sem],
                device_id={"row": row_peer(dists[at]), "col": col_at},
                device_id_type=MESH,
            )
        return to_rows

    def gram_copy(step, k):
        return pltpu.make_async_remote_copy(
            src_ref=gram_send[step],
            dst_ref=gram_recv[step].at[k],
            send_sem=g_send_sem.at[step, k],
            recv_sem=g_recv_sem.at[step, k],
            device_id=peer_of(k),
            device_id_type=MESH,
        )

    def publish(step, values):
        for v in range(vb):
            high = values[v].astype(jnp.bfloat16)
            low = (values[v] - high.astype(jnp.float32)).astype(jnp.bfloat16)
            for ref in (row_field[step], col_field[step]):
                ref[v, 0:width] = high
                ref[v, width : 2 * width] = low

    def product(values, tile, dim):
        both = matmul(values, tile, 1, dim)
        return both[0:width] + both[width : 2 * width]

    sent, arrived = {}, set()

    def start(copies):
        for key, copy in copies.items():
            copy.start()
            sent[key] = copy

    def arrive(copies):
        for key, copy in copies.items():
            copy.wait_recv()
            arrived.add(key)

    grams_sent, grams_in = [], []

    def start_grams(step):
        repeat(peers, lambda k: gram_copy(step, k).start())
        grams_sent.append(step)

    def scattered(targets, of):
        sums = []
        for target in range(targets):
            total = jnp.zeros((width, nodes), jnp.float32)
            for s in range(slots):
                total = total + jnp.where(of[s] == target, products[s], 0.0)
            sums.append(total)
        return sums

    def forward(step):
        arrive(field_to_rows(step))
        for s in range(slots):
            products[s] = product(col_field[step][col_at_index[s]], tiles[s], 1)
        for target, total in enumerate(scattered(nbr, row_of)):
            row_sum[target] = total
            row_send[step][target] = total.astype(SEND)
        start(parts_to_cols(step))

    def backward(step):
        arrive(field_to_cols(step))
        for s in range(slots):
            products[s] = product(row_field[step][row_at_index[s]], tiles[s], 0)
        sums = scattered(len(dists) * vb, col_of)
        for at in range(1, len(dists)):
            for v in range(vb):
                col_send[step][at - 1, v] = sums[at * vb + v].astype(SEND)
        start(parts_to_rows(step))
        return [sums[v] + row_sum[col_at * vb + v] for v in range(vb)]

    def combined(step, totals):
        arrive(parts_to_cols(step) | parts_to_rows(step))
        for k in range(n_col - 1):
            totals = [totals[v] + row_recv[step][k, v].astype(jnp.float32) for v in range(vb)]
        for at in range(len(dists) - 1):
            totals = [totals[v] + col_recv[step][at, v].astype(jnp.float32) for v in range(vb)]
        return totals

    def finish():
        for copy in sent.values():
            copy.wait_send()
        for step in grams_sent:
            repeat(peers, lambda k: gram_copy(step, k).wait_send())

    loads[0].wait()
    publish(0, field)
    pl.semaphore_wait(barrier, peers)
    start(field_to_rows(0) | field_to_cols(0))
    ahead = lax.broadcasted_iota(jnp.int32, (nodes, nodes), 1) - lax.broadcasted_iota(
        jnp.int32, (nodes, nodes), 0
    )
    loads[1].wait()
    for s in range(slots):
        loads[2 + s].wait()
        tiles[s] = jnp.where(ahead > limits[s], tiles[s], jnp.zeros_like(tiles[s]))
    forward(0)
    totals = combined(0, backward(0))
    for v in range(vb):
        image[v] = totals[v] + mass[v : v + 1, :] * field[v]

    publish(1, image)
    start(field_to_rows(1) | field_to_cols(1))

    def gram(first, second):
        total = None
        for v in range(vb):
            term = matmul(first[v], second[v], 1, 1, HIGHEST)
            total = term if total is None else total + term
        return total

    gram_send[0][:, 0:width] = gram(field, field)
    gram_send[0][:, width : 2 * width] = gram(field, image)
    gram_send[0][:, 2 * width : 3 * width] = gram(image, field)
    gram_send[0][:, 3 * width : 4 * width] = gram(image, image)
    start_grams(0)
    forward(1)
    totals = backward(1)

    def gathered(step):
        grams_in.append(step)
        repeat(peers, lambda k: gram_copy(step, k).wait_recv())
        total = gram_send[step][...]
        if peers <= 16:
            for k in range(peers):
                total = total + gram_recv[step][k]
            return total
        return lax.fori_loop(0, peers, lambda k, t: t + gram_recv[step][k], total)

    grams = gathered(0)
    norm = grams[:, 0:width]
    curv = grams[:, width : 2 * width]
    curv_t = grams[:, 2 * width : 3 * width]
    square = grams[:, 3 * width : 4 * width]
    unit = (
        lax.broadcasted_iota(jnp.int32, (width, width), 0)
        == lax.broadcasted_iota(jnp.int32, (width, width), 1)
    ).astype(jnp.float32)
    alpha, norm_inverse = eliminate([(0.5 * (curv + curv_t), norm), (norm, unit)])
    norm_next = (
        norm
        - matmul(curv, alpha, 1, 0, HIGHEST)
        - matmul(alpha, curv_t - matmul(square, alpha, 1, 0, HIGHEST), 0, 0, HIGHEST)
    )
    beta = matmul(norm_inverse, norm_next, 1, 0, HIGHEST)
    ahead_mix = unit + beta

    def mix(values, coef):
        return [matmul(coef, values[v], 0, 0, HIGHEST) for v in range(vb)]

    image_alpha = mix(image, alpha)
    field_alpha = mix(field, alpha)
    field_ahead = mix(field, ahead_mix)
    image_ahead = mix(image, ahead_mix)
    direction = [field_ahead[v] - image_alpha[v] for v in range(vb)]
    totals = combined(1, totals)
    second = [totals[v] + mass[v : v + 1, :] * image[v] for v in range(vb)]
    second_alpha = mix(second, alpha)
    image_next = [image_ahead[v] - second_alpha[v] for v in range(vb)]
    gram_send[1][:, 0:width] = 0.5 * (gram(direction, image_next) + gram(image_next, direction))
    start_grams(1)
    last = gathered(1)[:, 0:width]
    (alpha_next,) = eliminate([(last, norm_next)])
    direction_alpha = mix(direction, alpha_next)
    image_next_alpha = mix(image_next, alpha_next)
    for v in range(vb):
        solution_ref[v] = field_alpha[v] + direction_alpha[v]
        residual_ref[v] = (field[v] - image_alpha[v]) - image_next_alpha[v]

    finish()


def shards(probes, mass, blocks, slot_rows, slot_cols, slot_count):
    vb, width, nodes = probes.shape
    n_col = lax.axis_size("col")
    n_row = lax.axis_size("row")
    slots = blocks.shape[2]
    nbr = vb * n_col
    total_blocks = vb * n_col * n_row
    plane = total_blocks // 8
    offsets = [0, 1, 2, plane - 1, plane, plane + 1, 2 * plane]
    deltas = sorted(set([o // vb for o in offsets] + [(o + vb - 1) // vb for o in offsets]))
    dists = sorted(
        set(
            (first + d) // n_col
            for first in range(n_col)
            for d in deltas
            if (first + d) // n_col < n_row
        )
    )
    peers = n_row * n_col - 1
    low = jnp.bfloat16
    f32 = jnp.float32

    def twice(shape, dtype):
        return [pltpu.VMEM(shape, dtype), pltpu.VMEM(shape, dtype)]

    links = len(dists) - 1 + n_col - 1
    smem = pl.BlockSpec(memory_space=pltpu.SMEM)
    hbm = pl.BlockSpec(memory_space=pl.ANY)
    vmem = pl.BlockSpec(memory_space=pltpu.VMEM)
    out = jax.ShapeDtypeStruct((vb, width, nodes), f32)
    return pl.pallas_call(
        functools.partial(kernel, n_row, n_col, dists),
        out_shape=(out, out),
        in_specs=[hbm, hbm, hbm, smem, smem, smem],
        out_specs=(vmem, vmem),
        scratch_shapes=[
            pltpu.VMEM((vb, width, nodes), f32),
            pltpu.VMEM((vb, nodes), f32),
            pltpu.VMEM((slots, nodes, nodes), low),
            twice((nbr, 2 * width, nodes), low),
            twice((len(dists) * vb, 2 * width, nodes), low),
            pltpu.VMEM((slots, width, nodes), f32),
            pltpu.VMEM((nbr, width, nodes), f32),
            twice((nbr, width, nodes), SEND),
            twice((len(dists) - 1, vb, width, nodes), SEND),
            twice((n_col - 1, vb, width, nodes), SEND),
            twice((len(dists) - 1, vb, width, nodes), SEND),
            pltpu.VMEM((vb, width, nodes), f32),
            twice((width, 128), f32),
            twice((peers, width, 128), f32),
            pltpu.SemaphoreType.DMA((2 + slots,)),
            pltpu.SemaphoreType.DMA((2, links)),
            pltpu.SemaphoreType.DMA((2, links)),
            pltpu.SemaphoreType.DMA((2, links)),
            pltpu.SemaphoreType.DMA((2, links)),
            pltpu.SemaphoreType.DMA((2, peers)),
            pltpu.SemaphoreType.DMA((2, peers)),
        ],
        compiler_params=pltpu.CompilerParams(
            collective_id=0, has_side_effects=True, vmem_limit_bytes=60 * 1024 * 1024
        ),
    )(probes, mass, blocks, slot_rows, slot_cols, slot_count)


def solution(mesh):
    placed = (
        P(("grp", "row", "col"), None, None),
        P(("grp", "row", "col"), None),
        P(("grp", "row"), "col", None, None, None),
        P(("grp", "row"), "col", None),
        P(("grp", "row"), "col", None),
        P(("grp", "row"), "col"),
    )
    return jax.shard_map(
        shards,
        mesh=mesh,
        in_specs=placed,
        out_specs=(P(("grp", "row", "col"), None, None), P(("grp", "row", "col"), None, None)),
        check_vma=False,
    )
```

```python
import functools
import jax
import jax.numpy as jnp
from jax import lax
from jax.experimental import pallas as pl
from jax.experimental.pallas import tpu as pltpu
from jax.sharding import PartitionSpec as P

MESH = pl.DeviceIdType.MESH
HIGHEST = lax.Precision.HIGHEST
SEND = jnp.bfloat16


def matmul(a, b, a_dim, b_dim, precision=None):
    return lax.dot_general(
        a,
        b,
        (((a_dim,), (b_dim,)), ((), ())),
        precision=precision,
        preferred_element_type=jnp.float32,
    )


def repeat(count, body):
    if count <= 16:
        for k in range(count):
            body(k)
    else:
        lax.fori_loop(0, count, lambda k, c: (body(k), c)[1], 0)


def eliminate(systems):
    size = systems[0][0].shape[0]
    rows = lax.broadcasted_iota(jnp.int32, (size, 1), 0)
    for k in range(size):
        after = []
        for left, right in systems:
            left_k = left[k : k + 1, :]
            right_k = right[k : k + 1, :]
            inverse = 1.0 / left[k : k + 1, k : k + 1]
            left_k = left_k * inverse
            right_k = right_k * inverse
            factor = left[:, k : k + 1]
            here = rows == k
            after.append(
                (
                    jnp.where(here, left_k, left - factor * left_k),
                    jnp.where(here, right_k, right - factor * right_k),
                )
            )
        systems = after
    return [right for _, right in systems]


def kernel(
    n_row,
    n_col,
    dists,
    probes_hbm,
    mass_hbm,
    blocks_hbm,
    rows_ref,
    cols_ref,
    count_ref,
    solution_ref,
    residual_ref,
    field,
    mass,
    tiles,
    row_field,
    col_field,
    products,
    row_sum,
    row_send,
    col_send,
    row_recv,
    col_recv,
    image,
    gram_send,
    gram_recv,
    in_sem,
    a_send_sem,
    a_recv_sem,
    b_send_sem,
    b_recv_sem,
    g_send_sem,
    g_recv_sem,
):
    row_at = lax.axis_index("row")
    col_at = lax.axis_index("col")
    vb, width, nodes = field.shape
    slots = tiles.shape[0]
    nbr = vb * n_col
    peers = n_row * n_col - 1
    me = row_at * n_col + col_at

    def peer_of(k):
        at = lax.rem(me + k + 1, n_row * n_col)
        return {"row": at // n_col, "col": lax.rem(at, n_col)}

    def col_peer(k):
        return lax.rem(col_at + k, n_col)

    def row_peer(d):
        return lax.rem(row_at + d, n_row)

    loads = [
        pltpu.make_async_copy(probes_hbm, field, in_sem.at[0]),
        pltpu.make_async_copy(mass_hbm, mass, in_sem.at[1]),
    ]
    for s in range(slots):
        loads.append(pltpu.make_async_copy(blocks_hbm.at[0, 0, s], tiles.at[s], in_sem.at[2 + s]))
    for load in loads:
        load.start()

    barrier = pltpu.get_barrier_semaphore()

    near = [{"row": row_peer(k), "col": col_at} for k in range(1, n_row)]
    near += [{"row": row_at, "col": col_peer(k)} for k in range(1, n_col)]
    for peer in near:
        pl.semaphore_signal(barrier, inc=1, device_id=peer, device_id_type=MESH)

    live_count = count_ref[0, 0]
    limits, row_of, col_of, row_at_index, col_at_index = [], [], [], [], []
    for s in range(slots):
        live = s < live_count
        lrow = jnp.where(live, rows_ref[0, 0, s], 0)
        lcol = jnp.where(live, cols_ref[0, 0, s], row_at * vb)
        dist = lcol // vb - row_at
        place = jnp.int32(0)
        for at, d in enumerate(dists):
            place = place + jnp.where(dist == d, at, 0)
        part = lax.rem(lcol, vb)
        grow = row_at * nbr + lrow
        gcol = (lcol // vb * n_col + col_at) * vb + part
        limits.append(jnp.where(live, jnp.where(grow == gcol, 0, -nodes), nodes))
        row_of.append(lrow)
        col_of.append(place * vb + part)
        col_at_index.append(place * vb + part)
        row_at_index.append(
            lax.rem(col_at - lrow // vb + n_col, n_col) * vb + lax.rem(lrow, vb)
        )

    def field_to_rows(step):
        to_rows = {}
        for at in range(1, len(dists)):
            to_rows["fr", step, at] = pltpu.make_async_remote_copy(
                src_ref=col_field[step].at[pl.ds(0, vb)],
                dst_ref=col_field[step].at[pl.ds(at * vb, vb)],
                send_sem=a_send_sem.at[step, at - 1],
                recv_sem=a_recv_sem.at[step, at - 1],
                device_id={"row": row_peer(n_row - dists[at]), "col": col_at},
                device_id_type=MESH,
            )
        return to_rows

    def field_to_cols(step):
        to_cols = {}
        for k in range(1, n_col):
            sem = len(dists) - 2 + k
            to_cols["fc", step, k] = pltpu.make_async_remote_copy(
                src_ref=row_field[step].at[pl.ds(0, vb)],
                dst_ref=row_field[step].at[pl.ds(k * vb, vb)],
                send_sem=a_send_sem.at[step, sem],
                recv_sem=a_recv_sem.at[step, sem],
                device_id={"row": row_at, "col": col_peer(k)},
                device_id_type=MESH,
            )
        return to_cols

    def parts_to_cols(step):
        to_cols = {}
        for k in range(1, n_col):
            to_cols["pc", step, k] = pltpu.make_async_remote_copy(
                src_ref=row_send[step].at[pl.ds(col_peer(k) * vb, vb)],
                dst_ref=row_recv[step].at[k - 1],
                send_sem=b_send_sem.at[step, k - 1],
                recv_sem=b_recv_sem.at[step, k - 1],
                device_id={"row": row_at, "col": col_peer(k)},
                device_id_type=MESH,
            )
        return to_cols

    def parts_to_rows(step):
        to_rows = {}
        for at in range(1, len(dists)):
            sem = n_col - 2 + at
            to_rows["pr", step, at] = pltpu.make_async_remote_copy(
                src_ref=col_send[step].at[at - 1],
                dst_ref=col_recv[step].at[at - 1],
                send_sem=b_send_sem.at[step, sem],
                recv_sem=b_recv_sem.at[step, sem],
                device_id={"row": row_peer(dists[at]), "col": col_at},
                device_id_type=MESH,
            )
        return to_rows

    def gram_copy(step, k):
        return pltpu.make_async_remote_copy(
            src_ref=gram_send[step],
            dst_ref=gram_recv[step].at[k],
            send_sem=g_send_sem.at[step, k],
            recv_sem=g_recv_sem.at[step, k],
            device_id=peer_of(k),
            device_id_type=MESH,
        )

    def publish(step, values):
        for v in range(vb):
            high = values[v].astype(jnp.bfloat16)
            low = (values[v] - high.astype(jnp.float32)).astype(jnp.bfloat16)
            for ref in (row_field[step], col_field[step]):
                ref[v, 0:width] = high
                ref[v, width : 2 * width] = low

    def product(values, tile, dim):
        both = matmul(values, tile, 1, dim)
        return both[0:width] + both[width : 2 * width]

    sent, arrived = {}, set()

    def start(copies):
        for key, copy in copies.items():
            copy.start()
            sent[key] = copy

    def arrive(copies):
        for key, copy in copies.items():
            copy.wait_recv()
            arrived.add(key)

    grams_sent, grams_in = [], []

    def start_grams(step):
        repeat(peers, lambda k: gram_copy(step, k).start())
        grams_sent.append(step)

    def scattered(targets, of):
        sums = []
        for target in range(targets):
            total = jnp.zeros((width, nodes), jnp.float32)
            for s in range(slots):
                total = total + jnp.where(of[s] == target, products[s], 0.0)
            sums.append(total)
        return sums

    def forward(step):
        arrive(field_to_rows(step))
        for s in range(slots):
            products[s] = product(col_field[step][col_at_index[s]], tiles[s], 1)
        for target, total in enumerate(scattered(nbr, row_of)):
            row_sum[target] = total
            row_send[step][target] = total.astype(SEND)
        start(parts_to_cols(step))

    def backward(step):
        arrive(field_to_cols(step))
        for s in range(slots):
            products[s] = product(row_field[step][row_at_index[s]], tiles[s], 0)
        sums = scattered(len(dists) * vb, col_of)
        for at in range(1, len(dists)):
            for v in range(vb):
                col_send[step][at - 1, v] = sums[at * vb + v].astype(SEND)
        start(parts_to_rows(step))
        return [sums[v] + row_sum[col_at * vb + v] for v in range(vb)]

    def combined(step, totals):
        arrive(parts_to_cols(step) | parts_to_rows(step))
        for k in range(n_col - 1):
            totals = [totals[v] + row_recv[step][k, v].astype(jnp.float32) for v in range(vb)]
        for at in range(len(dists) - 1):
            totals = [totals[v] + col_recv[step][at, v].astype(jnp.float32) for v in range(vb)]
        return totals

    def finish():
        for copy in sent.values():
            copy.wait_send()
        for step in grams_sent:
            repeat(peers, lambda k: gram_copy(step, k).wait_send())

    loads[0].wait()
    publish(0, field)
    ahead = lax.broadcasted_iota(jnp.int32, (nodes, nodes), 1) - lax.broadcasted_iota(
        jnp.int32, (nodes, nodes), 0
    )
    loads[1].wait()
    for s in range(slots):
        loads[2 + s].wait()
        tiles[s] = jnp.where(ahead > limits[s], tiles[s], jnp.zeros_like(tiles[s]))
    pl.semaphore_wait(barrier, len(near))
    start(field_to_rows(0) | field_to_cols(0))
    forward(0)
    totals = combined(0, backward(0))
    for v in range(vb):
        image[v] = totals[v] + mass[v : v + 1, :] * field[v]

    publish(1, image)
    start(field_to_rows(1) | field_to_cols(1))

    def gram(first, second):
        total = None
        for v in range(vb):
            both = jnp.concatenate([first[v], second[v]], axis=0)
            term = matmul(both, both, 1, 1, HIGHEST)
            total = term if total is None else total + term
        return total

    groups = 2 * width // 8

    def pack(step, total):
        for g in range(groups):
            gram_send[step][:, 2 * width * g : 2 * width * (g + 1)] = total[8 * g : 8 * (g + 1)]

    def unpack(packed):
        total = jnp.concatenate(
            [packed[:, 2 * width * g : 2 * width * (g + 1)] for g in range(groups)], axis=0
        )
        upper, lower = total[0:width], total[width : 2 * width]
        return upper[:, 0:width], upper[:, width:], lower[:, 0:width], lower[:, width:]

    pack(0, gram(field, image))
    start_grams(0)
    forward(1)
    totals = backward(1)

    def gathered(step):
        grams_in.append(step)
        repeat(peers, lambda k: gram_copy(step, k).wait_recv())
        total = gram_send[step][...]
        if peers <= 16:
            for k in range(peers):
                total = total + gram_recv[step][k]
            return total
        return lax.fori_loop(0, peers, lambda k, t: t + gram_recv[step][k], total)

    grams = gathered(0)
    norm, curv, curv_t, square = unpack(grams)
    unit = (
        lax.broadcasted_iota(jnp.int32, (width, width), 0)
        == lax.broadcasted_iota(jnp.int32, (width, width), 1)
    ).astype(jnp.float32)
    alpha, norm_inverse = eliminate([(0.5 * (curv + curv_t), norm), (norm, unit)])
    norm_next = (
        norm
        - matmul(curv, alpha, 1, 0, HIGHEST)
        - matmul(alpha, curv_t - matmul(square, alpha, 1, 0, HIGHEST), 0, 0, HIGHEST)
    )
    beta = matmul(norm_inverse, norm_next, 1, 0, HIGHEST)
    ahead_mix = unit + beta

    def mix(values, coef):
        return [matmul(coef, values[v], 0, 0, HIGHEST) for v in range(vb)]

    image_alpha = mix(image, alpha)
    field_alpha = mix(field, alpha)
    field_ahead = mix(field, ahead_mix)
    image_ahead = mix(image, ahead_mix)
    direction = [field_ahead[v] - image_alpha[v] for v in range(vb)]
    known = gram(direction, image_ahead)
    known_turned = jnp.concatenate([known[:, width:], known[:, 0:width]], axis=1)
    totals = combined(1, totals)
    second = [totals[v] + mass[v : v + 1, :] * image[v] for v in range(vb)]
    fresh = gram(direction, second)
    first_half = lax.broadcasted_iota(jnp.int32, (2 * width, 2 * width), 0) < width
    left_half = lax.broadcasted_iota(jnp.int32, (2 * width, 2 * width), 1) < width
    pack(1, jnp.where(first_half == left_half, known_turned, fresh))
    start_grams(1)
    second_alpha = mix(second, alpha)
    image_next = [image_ahead[v] - second_alpha[v] for v in range(vb)]
    known_sum, fresh_sum, fresh_sum_t, known_sum_t = unpack(gathered(1))
    last = known_sum - matmul(fresh_sum, alpha, 1, 0, HIGHEST)
    last_t = known_sum_t - matmul(alpha, fresh_sum_t, 0, 0, HIGHEST)
    (alpha_next,) = eliminate([(0.5 * (last + last_t), norm_next)])
    direction_alpha = mix(direction, alpha_next)
    image_next_alpha = mix(image_next, alpha_next)
    for v in range(vb):
        solution_ref[v] = field_alpha[v] + direction_alpha[v]
        residual_ref[v] = (field[v] - image_alpha[v]) - image_next_alpha[v]

    finish()


def shards(probes, mass, blocks, slot_rows, slot_cols, slot_count):
    vb, width, nodes = probes.shape
    n_col = lax.axis_size("col")
    n_row = lax.axis_size("row")
    slots = blocks.shape[2]
    nbr = vb * n_col
    total_blocks = vb * n_col * n_row
    plane = total_blocks // 8
    offsets = [0, 1, 2, plane - 1, plane, plane + 1, 2 * plane]
    deltas = sorted(set([o // vb for o in offsets] + [(o + vb - 1) // vb for o in offsets]))
    dists = sorted(
        set(
            (first + d) // n_col
            for first in range(n_col)
            for d in deltas
            if (first + d) // n_col < n_row
        )
    )
    peers = n_row * n_col - 1
    low = jnp.bfloat16
    f32 = jnp.float32

    def twice(shape, dtype):
        return [pltpu.VMEM(shape, dtype), pltpu.VMEM(shape, dtype)]

    links = len(dists) - 1 + n_col - 1
    smem = pl.BlockSpec(memory_space=pltpu.SMEM)
    hbm = pl.BlockSpec(memory_space=pl.ANY)
    vmem = pl.BlockSpec(memory_space=pltpu.VMEM)
    out = jax.ShapeDtypeStruct((vb, width, nodes), f32)
    return pl.pallas_call(
        functools.partial(kernel, n_row, n_col, dists),
        out_shape=(out, out),
        in_specs=[hbm, hbm, hbm, smem, smem, smem],
        out_specs=(vmem, vmem),
        scratch_shapes=[
            pltpu.VMEM((vb, width, nodes), f32),
            pltpu.VMEM((vb, nodes), f32),
            pltpu.VMEM((slots, nodes, nodes), low),
            twice((nbr, 2 * width, nodes), low),
            twice((len(dists) * vb, 2 * width, nodes), low),
            pltpu.VMEM((slots, width, nodes), f32),
            pltpu.VMEM((nbr, width, nodes), f32),
            twice((nbr, width, nodes), SEND),
            twice((len(dists) - 1, vb, width, nodes), SEND),
            twice((n_col - 1, vb, width, nodes), SEND),
            twice((len(dists) - 1, vb, width, nodes), SEND),
            pltpu.VMEM((vb, width, nodes), f32),
            twice((8, 4 * width * width // 8), f32),
            twice((peers, 8, 4 * width * width // 8), f32),
            pltpu.SemaphoreType.DMA((2 + slots,)),
            pltpu.SemaphoreType.DMA((2, links)),
            pltpu.SemaphoreType.DMA((2, links)),
            pltpu.SemaphoreType.DMA((2, links)),
            pltpu.SemaphoreType.DMA((2, links)),
            pltpu.SemaphoreType.DMA((2, peers)),
            pltpu.SemaphoreType.DMA((2, peers)),
        ],
        compiler_params=pltpu.CompilerParams(
            collective_id=0, has_side_effects=True, vmem_limit_bytes=60 * 1024 * 1024
        ),
    )(probes, mass, blocks, slot_rows, slot_cols, slot_count)


def solution(mesh):
    placed = (
        P(("grp", "row", "col"), None, None),
        P(("grp", "row", "col"), None),
        P(("grp", "row"), "col", None, None, None),
        P(("grp", "row"), "col", None),
        P(("grp", "row"), "col", None),
        P(("grp", "row"), "col"),
    )
    return jax.shard_map(
        shards,
        mesh=mesh,
        in_specs=placed,
        out_specs=(P(("grp", "row", "col"), None, None), P(("grp", "row", "col"), None, None)),
        check_vma=False,
    )
```

```python
import functools
import jax
import jax.numpy as jnp
from jax import lax
from jax.experimental import pallas as pl
from jax.experimental.pallas import tpu as pltpu
from jax.sharding import PartitionSpec as P

MESH = pl.DeviceIdType.MESH
HIGHEST = lax.Precision.HIGHEST
SEND = jnp.bfloat16


def matmul(a, b, a_dim, b_dim, precision=None):
    return lax.dot_general(
        a,
        b,
        (((a_dim,), (b_dim,)), ((), ())),
        precision=precision,
        preferred_element_type=jnp.float32,
    )


def repeat(count, body):
    if count <= 16:
        for k in range(count):
            body(k)
    else:
        lax.fori_loop(0, count, lambda k, c: (body(k), c)[1], 0)


def eliminate(systems):
    size = systems[0][0].shape[0]
    rows = lax.broadcasted_iota(jnp.int32, (size, 1), 0)
    for k in range(size):
        after = []
        for left, right in systems:
            left_k = left[k : k + 1, :]
            right_k = right[k : k + 1, :]
            inverse = 1.0 / left[k : k + 1, k : k + 1]
            left_k = left_k * inverse
            right_k = right_k * inverse
            factor = left[:, k : k + 1]
            here = rows == k
            after.append(
                (
                    jnp.where(here, left_k, left - factor * left_k),
                    jnp.where(here, right_k, right - factor * right_k),
                )
            )
        systems = after
    return [right for _, right in systems]


def kernel(
    n_row,
    n_col,
    dists,
    probes_hbm,
    mass_hbm,
    blocks_hbm,
    rows_ref,
    cols_ref,
    count_ref,
    solution_ref,
    residual_ref,
    field,
    mass,
    tiles,
    row_field,
    col_field,
    products,
    row_sum,
    row_send,
    col_send,
    row_recv,
    col_recv,
    image,
    gram_send,
    gram_recv,
    in_sem,
    a_send_sem,
    a_recv_sem,
    b_send_sem,
    b_recv_sem,
    g_send_sem,
    g_recv_sem,
):
    row_at = lax.axis_index("row")
    col_at = lax.axis_index("col")
    vb, width, nodes = field.shape
    slots = tiles.shape[0]
    nbr = vb * n_col
    peers = n_row * n_col - 1
    me = row_at * n_col + col_at

    def peer_of(k):
        at = lax.rem(me + k + 1, n_row * n_col)
        return {"row": at // n_col, "col": lax.rem(at, n_col)}

    def col_peer(k):
        return lax.rem(col_at + k, n_col)

    def row_peer(d):
        return lax.rem(row_at + d, n_row)

    loads = [
        pltpu.make_async_copy(probes_hbm, field, in_sem.at[0]),
        pltpu.make_async_copy(mass_hbm, mass, in_sem.at[1]),
    ]
    for s in range(slots):
        loads.append(pltpu.make_async_copy(blocks_hbm.at[0, 0, s], tiles.at[s], in_sem.at[2 + s]))
    for load in loads:
        load.start()

    barrier = pltpu.get_barrier_semaphore()

    near = [{"row": row_peer(k), "col": col_at} for k in range(1, n_row)]
    near += [{"row": row_at, "col": col_peer(k)} for k in range(1, n_col)]
    for peer in near:
        pl.semaphore_signal(barrier, inc=1, device_id=peer, device_id_type=MESH)

    live_count = count_ref[0, 0]
    limits, row_of, col_of, row_at_index, col_at_index = [], [], [], [], []
    for s in range(slots):
        live = s < live_count
        lrow = jnp.where(live, rows_ref[0, 0, s], 0)
        lcol = jnp.where(live, cols_ref[0, 0, s], row_at * vb)
        dist = lcol // vb - row_at
        place = jnp.int32(0)
        for at, d in enumerate(dists):
            place = place + jnp.where(dist == d, at, 0)
        part = lax.rem(lcol, vb)
        grow = row_at * nbr + lrow
        gcol = (lcol // vb * n_col + col_at) * vb + part
        limits.append(jnp.where(live, jnp.where(grow == gcol, 0, -nodes), nodes))
        row_of.append(lrow)
        col_of.append(place * vb + part)
        col_at_index.append(place * vb + part)
        row_at_index.append(
            lax.rem(col_at - lrow // vb + n_col, n_col) * vb + lax.rem(lrow, vb)
        )

    def field_to_rows(step):
        to_rows = {}
        for at in range(1, len(dists)):
            to_rows["fr", step, at] = pltpu.make_async_remote_copy(
                src_ref=col_field[step].at[pl.ds(0, vb)],
                dst_ref=col_field[step].at[pl.ds(at * vb, vb)],
                send_sem=a_send_sem.at[step, at - 1],
                recv_sem=a_recv_sem.at[step, at - 1],
                device_id={"row": row_peer(n_row - dists[at]), "col": col_at},
                device_id_type=MESH,
            )
        return to_rows

    def field_to_cols(step):
        to_cols = {}
        for k in range(1, n_col):
            sem = len(dists) - 2 + k
            to_cols["fc", step, k] = pltpu.make_async_remote_copy(
                src_ref=row_field[step].at[pl.ds(0, vb)],
                dst_ref=row_field[step].at[pl.ds(k * vb, vb)],
                send_sem=a_send_sem.at[step, sem],
                recv_sem=a_recv_sem.at[step, sem],
                device_id={"row": row_at, "col": col_peer(k)},
                device_id_type=MESH,
            )
        return to_cols

    def parts_to_cols(step):
        to_cols = {}
        for k in range(1, n_col):
            to_cols["pc", step, k] = pltpu.make_async_remote_copy(
                src_ref=row_send[step].at[pl.ds(col_peer(k) * vb, vb)],
                dst_ref=row_recv[step].at[k - 1],
                send_sem=b_send_sem.at[step, k - 1],
                recv_sem=b_recv_sem.at[step, k - 1],
                device_id={"row": row_at, "col": col_peer(k)},
                device_id_type=MESH,
            )
        return to_cols

    def parts_to_rows(step):
        to_rows = {}
        for at in range(1, len(dists)):
            sem = n_col - 2 + at
            to_rows["pr", step, at] = pltpu.make_async_remote_copy(
                src_ref=col_send[step].at[at - 1],
                dst_ref=col_recv[step].at[at - 1],
                send_sem=b_send_sem.at[step, sem],
                recv_sem=b_recv_sem.at[step, sem],
                device_id={"row": row_peer(dists[at]), "col": col_at},
                device_id_type=MESH,
            )
        return to_rows

    def gram_copy(step, k):
        return pltpu.make_async_remote_copy(
            src_ref=gram_send[step],
            dst_ref=gram_recv[step].at[k],
            send_sem=g_send_sem.at[step, k],
            recv_sem=g_recv_sem.at[step, k],
            device_id=peer_of(k),
            device_id_type=MESH,
        )

    def publish(step, values):
        for v in range(vb):
            high = values[v].astype(jnp.bfloat16)
            low = (values[v] - high.astype(jnp.float32)).astype(jnp.bfloat16)
            for ref in (row_field[step], col_field[step]):
                ref[v, 0:width] = high
                ref[v, width : 2 * width] = low

    def product(values, tile, dim):
        both = matmul(values, tile, 1, dim)
        return both[0:width] + both[width : 2 * width]

    sent, arrived = {}, set()

    def start(copies):
        for key, copy in copies.items():
            copy.start()
            sent[key] = copy

    def arrive(copies):
        for key, copy in copies.items():
            copy.wait_recv()
            arrived.add(key)

    grams_sent, grams_in = [], []

    def start_grams(step):
        repeat(peers, lambda k: gram_copy(step, k).start())
        grams_sent.append(step)

    def scattered(targets, of):
        sums = []
        for target in range(targets):
            total = jnp.zeros((width, nodes), jnp.float32)
            for s in range(slots):
                total = total + jnp.where(of[s] == target, products[s], 0.0)
            sums.append(total)
        return sums

    def forward(step):
        arrive(field_to_rows(step))
        for s in range(slots):
            products[s] = product(col_field[step][col_at_index[s]], tiles[s], 1)
        for target, total in enumerate(scattered(nbr, row_of)):
            row_sum[target] = total
            row_send[step][target] = total.astype(SEND)
        start(parts_to_cols(step))

    def backward(step):
        arrive(field_to_cols(step))
        for s in range(slots):
            products[s] = product(row_field[step][row_at_index[s]], tiles[s], 0)
        sums = scattered(len(dists) * vb, col_of)
        for at in range(1, len(dists)):
            for v in range(vb):
                col_send[step][at - 1, v] = sums[at * vb + v].astype(SEND)
        start(parts_to_rows(step))
        return [sums[v] + row_sum[col_at * vb + v] for v in range(vb)]

    def combined(step, totals):
        arrive(parts_to_cols(step) | parts_to_rows(step))
        for k in range(n_col - 1):
            totals = [totals[v] + row_recv[step][k, v].astype(jnp.float32) for v in range(vb)]
        for at in range(len(dists) - 1):
            totals = [totals[v] + col_recv[step][at, v].astype(jnp.float32) for v in range(vb)]
        return totals

    def finish():
        for copy in sent.values():
            copy.wait_send()
        for step in grams_sent:
            repeat(peers, lambda k: gram_copy(step, k).wait_send())

    loads[0].wait()
    publish(0, field)
    ahead = lax.broadcasted_iota(jnp.int32, (nodes, nodes), 1) - lax.broadcasted_iota(
        jnp.int32, (nodes, nodes), 0
    )
    loads[1].wait()
    for s in range(slots):
        loads[2 + s].wait()
        tiles[s] = jnp.where(ahead > limits[s], tiles[s], jnp.zeros_like(tiles[s]))
    pl.semaphore_wait(barrier, len(near))
    start(field_to_rows(0) | field_to_cols(0))
    forward(0)
    totals = combined(0, backward(0))
    for v in range(vb):
        image[v] = totals[v] + mass[v : v + 1, :] * field[v]

    publish(1, image)
    start(field_to_rows(1) | field_to_cols(1))

    def gram(first, second):
        total = None
        for v in range(vb):
            both = jnp.concatenate([first[v], second[v]], axis=0)
            term = matmul(both, both, 1, 1, HIGHEST)
            total = term if total is None else total + term
        return total

    groups = 2 * width // 8

    def pack(step, total):
        for g in range(groups):
            gram_send[step][:, 2 * width * g : 2 * width * (g + 1)] = total[8 * g : 8 * (g + 1)]

    def unpack(packed):
        total = jnp.concatenate(
            [packed[:, 2 * width * g : 2 * width * (g + 1)] for g in range(groups)], axis=0
        )
        upper, lower = total[0:width], total[width : 2 * width]
        return upper[:, 0:width], upper[:, width:], lower[:, 0:width], lower[:, width:]

    pack(0, gram(field, image))
    forward(1)
    start_grams(0)
    totals = backward(1)
    totals = combined(1, totals)
    second = [totals[v] + mass[v : v + 1, :] * image[v] for v in range(vb)]
    tall, wide = None, None
    for v in range(vb):
        both = jnp.concatenate([field[v], image[v]], axis=0)
        down = matmul(both, second[v], 1, 1, HIGHEST)
        across = matmul(second[v], both, 1, 1, HIGHEST)
        tall = down if tall is None else tall + down
        wide = across if wide is None else wide + across
    for g in range(groups):
        gram_send[1][:, width * g : width * (g + 1)] = tall[8 * g : 8 * (g + 1)]
    for g in range(groups // 2):
        at = groups * width + 2 * width * g
        gram_send[1][:, at : at + 2 * width] = wide[8 * g : 8 * (g + 1)]
    start_grams(1)

    def gathered(step):
        grams_in.append(step)
        repeat(peers, lambda k: gram_copy(step, k).wait_recv())
        total = gram_send[step][...]
        if peers <= 16:
            for k in range(peers):
                total = total + gram_recv[step][k]
            return total
        return lax.fori_loop(0, peers, lambda k, t: t + gram_recv[step][k], total)

    grams = gathered(0)
    norm, curv, curv_t, square = unpack(grams)
    unit = (
        lax.broadcasted_iota(jnp.int32, (width, width), 0)
        == lax.broadcasted_iota(jnp.int32, (width, width), 1)
    ).astype(jnp.float32)
    alpha, norm_inverse = eliminate([(0.5 * (curv + curv_t), norm), (norm, unit)])
    norm_next = (
        norm
        - matmul(curv, alpha, 1, 0, HIGHEST)
        - matmul(alpha, curv_t - matmul(square, alpha, 1, 0, HIGHEST), 0, 0, HIGHEST)
    )
    beta = matmul(norm_inverse, norm_next, 1, 0, HIGHEST)
    ahead_mix = unit + beta

    def mix(values, coef):
        return [matmul(coef, values[v], 0, 0, HIGHEST) for v in range(vb)]

    image_alpha = mix(image, alpha)
    field_alpha = mix(field, alpha)
    field_ahead = mix(field, ahead_mix)
    image_ahead = mix(image, ahead_mix)
    direction = [field_ahead[v] - image_alpha[v] for v in range(vb)]
    second_alpha = mix(second, alpha)
    image_next = [image_ahead[v] - second_alpha[v] for v in range(vb)]
    direction_image = matmul(ahead_mix, curv, 0, 0, HIGHEST) - matmul(
        alpha, square, 0, 0, HIGHEST
    )
    image_direction = matmul(curv_t, ahead_mix, 1, 0, HIGHEST) - matmul(
        square, alpha, 1, 0, HIGHEST
    )
    known = matmul(direction_image, ahead_mix, 1, 0, HIGHEST)
    known_t = matmul(ahead_mix, image_direction, 0, 0, HIGHEST)
    weights = jnp.concatenate([ahead_mix, -alpha], axis=0)
    packed = gathered(1)
    tall = jnp.concatenate(
        [packed[:, width * g : width * (g + 1)] for g in range(groups)], axis=0
    )
    wide = jnp.concatenate(
        [
            packed[:, groups * width + 2 * width * g : groups * width + 2 * width * (g + 1)]
            for g in range(groups // 2)
        ],
        axis=0,
    )
    last = known - matmul(matmul(weights, tall, 0, 0, HIGHEST), alpha, 1, 0, HIGHEST)
    last_t = known_t - matmul(alpha, matmul(wide, weights, 1, 0, HIGHEST), 0, 0, HIGHEST)
    (alpha_next,) = eliminate([(0.5 * (last + last_t), norm_next)])
    direction_alpha = mix(direction, alpha_next)
    image_next_alpha = mix(image_next, alpha_next)
    for v in range(vb):
        solution_ref[v] = field_alpha[v] + direction_alpha[v]
        residual_ref[v] = (field[v] - image_alpha[v]) - image_next_alpha[v]

    finish()


def shards(probes, mass, blocks, slot_rows, slot_cols, slot_count):
    vb, width, nodes = probes.shape
    n_col = lax.axis_size("col")
    n_row = lax.axis_size("row")
    slots = blocks.shape[2]
    nbr = vb * n_col
    total_blocks = vb * n_col * n_row
    plane = total_blocks // 8
    offsets = [0, 1, 2, plane - 1, plane, plane + 1, 2 * plane]
    deltas = sorted(set([o // vb for o in offsets] + [(o + vb - 1) // vb for o in offsets]))
    dists = sorted(
        set(
            (first + d) // n_col
            for first in range(n_col)
            for d in deltas
            if (first + d) // n_col < n_row
        )
    )
    peers = n_row * n_col - 1
    low = jnp.bfloat16
    f32 = jnp.float32

    def twice(shape, dtype):
        return [pltpu.VMEM(shape, dtype), pltpu.VMEM(shape, dtype)]

    links = len(dists) - 1 + n_col - 1
    smem = pl.BlockSpec(memory_space=pltpu.SMEM)
    hbm = pl.BlockSpec(memory_space=pltpu.HBM)
    vmem = pl.BlockSpec(memory_space=pltpu.VMEM)
    out = jax.ShapeDtypeStruct((vb, width, nodes), f32)
    return pl.pallas_call(
        functools.partial(kernel, n_row, n_col, dists),
        out_shape=(out, out),
        in_specs=[hbm, hbm, hbm, smem, smem, smem],
        out_specs=(vmem, vmem),
        scratch_shapes=[
            pltpu.VMEM((vb, width, nodes), f32),
            pltpu.VMEM((vb, nodes), f32),
            pltpu.VMEM((slots, nodes, nodes), low),
            twice((nbr, 2 * width, nodes), low),
            twice((len(dists) * vb, 2 * width, nodes), low),
            pltpu.VMEM((slots, width, nodes), f32),
            pltpu.VMEM((nbr, width, nodes), f32),
            twice((nbr, width, nodes), SEND),
            twice((len(dists) - 1, vb, width, nodes), SEND),
            twice((n_col - 1, vb, width, nodes), SEND),
            twice((len(dists) - 1, vb, width, nodes), SEND),
            pltpu.VMEM((vb, width, nodes), f32),
            twice((8, 4 * width * width // 8), f32),
            twice((peers, 8, 4 * width * width // 8), f32),
            pltpu.SemaphoreType.DMA((2 + slots,)),
            pltpu.SemaphoreType.DMA((2, links)),
            pltpu.SemaphoreType.DMA((2, links)),
            pltpu.SemaphoreType.DMA((2, links)),
            pltpu.SemaphoreType.DMA((2, links)),
            pltpu.SemaphoreType.DMA((2, peers)),
            pltpu.SemaphoreType.DMA((2, peers)),
        ],
        compiler_params=pltpu.CompilerParams(
            collective_id=0, has_side_effects=True, vmem_limit_bytes=32 * 1024 * 1024
        ),
    )(probes, mass, blocks, slot_rows, slot_cols, slot_count)


def solution(mesh):
    placed = (
        P(("grp", "row", "col"), None, None),
        P(("grp", "row", "col"), None),
        P(("grp", "row"), "col", None, None, None),
        P(("grp", "row"), "col", None),
        P(("grp", "row"), "col", None),
        P(("grp", "row"), "col"),
    )
    return jax.shard_map(
        shards,
        mesh=mesh,
        in_specs=placed,
        out_specs=(P(("grp", "row", "col"), None, None), P(("grp", "row", "col"), None, None)),
        check_vma=False,
    )
```

```python
import functools
import jax
import jax.numpy as jnp
from jax import lax
from jax.experimental import pallas as pl
from jax.experimental.pallas import tpu as pltpu
from jax.sharding import PartitionSpec as P

MESH = pl.DeviceIdType.MESH
HIGHEST = lax.Precision.HIGHEST
SEND = jnp.bfloat16


def matmul(a, b, a_dim, b_dim, precision=None):
    return lax.dot_general(
        a,
        b,
        (((a_dim,), (b_dim,)), ((), ())),
        precision=precision,
        preferred_element_type=jnp.float32,
    )


def repeat(count, body):
    if count <= 16:
        for k in range(count):
            body(k)
    else:
        lax.fori_loop(0, count, lambda k, c: (body(k), c)[1], 0)


def eliminate(systems):
    size = systems[0][0].shape[0]
    rows = lax.broadcasted_iota(jnp.int32, (size, 1), 0)
    for k in range(size):
        after = []
        for left, right in systems:
            left_k = left[k : k + 1, :]
            right_k = right[k : k + 1, :]
            inverse = 1.0 / left[k : k + 1, k : k + 1]
            left_k = left_k * inverse
            right_k = right_k * inverse
            factor = left[:, k : k + 1]
            here = rows == k
            after.append(
                (
                    jnp.where(here, left_k, left - factor * left_k),
                    jnp.where(here, right_k, right - factor * right_k),
                )
            )
        systems = after
    return [right for _, right in systems]


def kernel(
    n_row,
    n_col,
    dists,
    probes_hbm,
    mass_hbm,
    blocks_hbm,
    rows_ref,
    cols_ref,
    count_ref,
    solution_ref,
    residual_ref,
    field,
    mass,
    tiles,
    row_field,
    col_field,
    products,
    row_sum,
    row_send,
    col_send,
    row_recv,
    col_recv,
    image,
    gram_send,
    gram_recv,
    in_sem,
    a_send_sem,
    a_recv_sem,
    b_send_sem,
    b_recv_sem,
    g_send_sem,
    g_recv_sem,
):
    row_at = lax.axis_index("row")
    col_at = lax.axis_index("col")
    vb, width, nodes = field.shape
    slots = tiles.shape[0]
    nbr = vb * n_col
    peers = n_row * n_col - 1
    me = row_at * n_col + col_at

    def peer_of(k):
        at = lax.rem(me + k + 1, n_row * n_col)
        return {"row": at // n_col, "col": lax.rem(at, n_col)}

    def col_peer(k):
        return lax.rem(col_at + k, n_col)

    def row_peer(d):
        return lax.rem(row_at + d, n_row)

    loads = [
        pltpu.make_async_copy(probes_hbm, field, in_sem.at[0]),
        pltpu.make_async_copy(mass_hbm, mass, in_sem.at[1]),
    ]
    for s in range(slots):
        loads.append(pltpu.make_async_copy(blocks_hbm.at[0, 0, s], tiles.at[s], in_sem.at[2 + s]))
    for load in loads:
        load.start()

    barrier = pltpu.get_barrier_semaphore()

    near = [{"row": row_peer(k), "col": col_at} for k in range(1, n_row)]
    near += [{"row": row_at, "col": col_peer(k)} for k in range(1, n_col)]
    for peer in near:
        pl.semaphore_signal(barrier, inc=1, device_id=peer, device_id_type=MESH)

    live_count = count_ref[0, 0]
    limits, row_of, col_of, row_at_index, col_at_index = [], [], [], [], []
    for s in range(slots):
        live = s < live_count
        lrow = jnp.where(live, rows_ref[0, 0, s], 0)
        lcol = jnp.where(live, cols_ref[0, 0, s], row_at * vb)
        dist = lcol // vb - row_at
        place = jnp.int32(0)
        for at, d in enumerate(dists):
            place = place + jnp.where(dist == d, at, 0)
        part = lax.rem(lcol, vb)
        grow = row_at * nbr + lrow
        gcol = (lcol // vb * n_col + col_at) * vb + part
        limits.append(jnp.where(live, jnp.where(grow == gcol, 0, -nodes), nodes))
        row_of.append(lrow)
        col_of.append(place * vb + part)
        col_at_index.append(place * vb + part)
        row_at_index.append(
            lax.rem(col_at - lrow // vb + n_col, n_col) * vb + lax.rem(lrow, vb)
        )

    def field_to_rows(step):
        to_rows = {}
        for at in range(1, len(dists)):
            to_rows["fr", step, at] = pltpu.make_async_remote_copy(
                src_ref=col_field[step].at[pl.ds(0, vb)],
                dst_ref=col_field[step].at[pl.ds(at * vb, vb)],
                send_sem=a_send_sem.at[step, at - 1],
                recv_sem=a_recv_sem.at[step, at - 1],
                device_id={"row": row_peer(n_row - dists[at]), "col": col_at},
                device_id_type=MESH,
            )
        return to_rows

    def field_to_cols(step):
        to_cols = {}
        for k in range(1, n_col):
            sem = len(dists) - 2 + k
            to_cols["fc", step, k] = pltpu.make_async_remote_copy(
                src_ref=row_field[step].at[pl.ds(0, vb)],
                dst_ref=row_field[step].at[pl.ds(k * vb, vb)],
                send_sem=a_send_sem.at[step, sem],
                recv_sem=a_recv_sem.at[step, sem],
                device_id={"row": row_at, "col": col_peer(k)},
                device_id_type=MESH,
            )
        return to_cols

    def parts_to_cols(step):
        to_cols = {}
        for k in range(1, n_col):
            to_cols["pc", step, k] = pltpu.make_async_remote_copy(
                src_ref=row_send[step].at[pl.ds(col_peer(k) * vb, vb)],
                dst_ref=row_recv[step].at[k - 1],
                send_sem=b_send_sem.at[step, k - 1],
                recv_sem=b_recv_sem.at[step, k - 1],
                device_id={"row": row_at, "col": col_peer(k)},
                device_id_type=MESH,
            )
        return to_cols

    def parts_to_rows(step):
        to_rows = {}
        for at in range(1, len(dists)):
            sem = n_col - 2 + at
            to_rows["pr", step, at] = pltpu.make_async_remote_copy(
                src_ref=col_send[step].at[at - 1],
                dst_ref=col_recv[step].at[at - 1],
                send_sem=b_send_sem.at[step, sem],
                recv_sem=b_recv_sem.at[step, sem],
                device_id={"row": row_peer(dists[at]), "col": col_at},
                device_id_type=MESH,
            )
        return to_rows

    def gram_copy(step, k):
        return pltpu.make_async_remote_copy(
            src_ref=gram_send[step],
            dst_ref=gram_recv[step].at[k],
            send_sem=g_send_sem.at[step, k],
            recv_sem=g_recv_sem.at[step, k],
            device_id=peer_of(k),
            device_id_type=MESH,
        )

    def publish(step, values):
        for v in range(vb):
            high = values[v].astype(jnp.bfloat16)
            low = (values[v] - high.astype(jnp.float32)).astype(jnp.bfloat16)
            for ref in (row_field[step], col_field[step]):
                ref[v, 0:width] = high
                ref[v, width : 2 * width] = low

    def product(values, tile, dim):
        both = matmul(values, tile, 1, dim)
        return both[0:width] + both[width : 2 * width]

    sent, arrived = {}, set()

    def start(copies):
        for key, copy in copies.items():
            copy.start()
            sent[key] = copy

    def arrive(copies):
        for key, copy in copies.items():
            copy.wait_recv()
            arrived.add(key)

    grams_sent, grams_in = [], []

    def start_grams(step):
        repeat(peers, lambda k: gram_copy(step, k).start())
        grams_sent.append(step)

    def scattered(targets, of):
        sums = []
        for target in range(targets):
            total = jnp.zeros((width, nodes), jnp.float32)
            for s in range(slots):
                total = total + jnp.where(of[s] == target, products[s], 0.0)
            sums.append(total)
        return sums

    def forward(step):
        arrive(field_to_rows(step))
        for s in range(slots):
            products[s] = product(col_field[step][col_at_index[s]], tiles[s], 1)
        for target, total in enumerate(scattered(nbr, row_of)):
            row_sum[target] = total
            row_send[step][target] = total.astype(SEND)
        start(parts_to_cols(step))

    def backward(step):
        arrive(field_to_cols(step))
        for s in range(slots):
            products[s] = product(row_field[step][row_at_index[s]], tiles[s], 0)
        sums = scattered(len(dists) * vb, col_of)
        for at in range(1, len(dists)):
            for v in range(vb):
                col_send[step][at - 1, v] = sums[at * vb + v].astype(SEND)
        start(parts_to_rows(step))
        return [sums[v] + row_sum[col_at * vb + v] for v in range(vb)]

    def combined(step, totals):
        arrive(parts_to_cols(step) | parts_to_rows(step))
        for k in range(n_col - 1):
            totals = [totals[v] + row_recv[step][k, v].astype(jnp.float32) for v in range(vb)]
        for at in range(len(dists) - 1):
            totals = [totals[v] + col_recv[step][at, v].astype(jnp.float32) for v in range(vb)]
        return totals

    def finish():
        for copy in sent.values():
            copy.wait_send()
        for step in grams_sent:
            repeat(peers, lambda k: gram_copy(step, k).wait_send())

    loads[0].wait()
    publish(0, field)
    ahead = lax.broadcasted_iota(jnp.int32, (nodes, nodes), 1) - lax.broadcasted_iota(
        jnp.int32, (nodes, nodes), 0
    )
    loads[1].wait()
    for s in range(slots):
        loads[2 + s].wait()
        tiles[s] = jnp.where(ahead > limits[s], tiles[s], jnp.zeros_like(tiles[s]))
    pl.semaphore_wait(barrier, len(near))
    start(field_to_rows(0) | field_to_cols(0))
    forward(0)
    totals = combined(0, backward(0))
    for v in range(vb):
        image[v] = totals[v] + mass[v : v + 1, :] * field[v]

    publish(1, image)
    start(field_to_rows(1) | field_to_cols(1))

    def gram(first, second):
        total = None
        for v in range(vb):
            both = jnp.concatenate([first[v], second[v]], axis=0)
            term = matmul(both, both, 1, 1, HIGHEST)
            total = term if total is None else total + term
        return total

    groups = 2 * width // 8

    def pack(step, total):
        for g in range(groups):
            gram_send[step][:, 2 * width * g : 2 * width * (g + 1)] = total[8 * g : 8 * (g + 1)]

    def unpack(packed):
        total = jnp.concatenate(
            [packed[:, 2 * width * g : 2 * width * (g + 1)] for g in range(groups)], axis=0
        )
        upper, lower = total[0:width], total[width : 2 * width]
        return upper[:, 0:width], upper[:, width:], lower[:, 0:width], lower[:, width:]

    pack(0, gram(field, image))
    forward(1)
    start_grams(0)
    totals = backward(1)
    totals = combined(1, totals)
    second = [totals[v] + mass[v : v + 1, :] * image[v] for v in range(vb)]
    tall, wide = None, None
    for v in range(vb):
        both = jnp.concatenate([field[v], image[v]], axis=0)
        down = matmul(both, second[v], 1, 1, HIGHEST)
        across = matmul(second[v], both, 1, 1, HIGHEST)
        tall = down if tall is None else tall + down
        wide = across if wide is None else wide + across
    for g in range(groups):
        gram_send[1][:, width * g : width * (g + 1)] = tall[8 * g : 8 * (g + 1)]
    for g in range(groups // 2):
        at = groups * width + 2 * width * g
        gram_send[1][:, at : at + 2 * width] = wide[8 * g : 8 * (g + 1)]
    start_grams(1)

    def gathered(step):
        grams_in.append(step)
        repeat(peers, lambda k: gram_copy(step, k).wait_recv())
        total = gram_send[step][...]
        if peers <= 16:
            for k in range(peers):
                total = total + gram_recv[step][k]
            return total
        return lax.fori_loop(0, peers, lambda k, t: t + gram_recv[step][k], total)

    grams = gathered(0)
    norm, curv, curv_t, square = unpack(grams)
    unit = (
        lax.broadcasted_iota(jnp.int32, (width, width), 0)
        == lax.broadcasted_iota(jnp.int32, (width, width), 1)
    ).astype(jnp.float32)
    alpha, norm_inverse = eliminate([(0.5 * (curv + curv_t), norm), (norm, unit)])
    norm_next = (
        norm
        - matmul(curv, alpha, 1, 0, HIGHEST)
        - matmul(alpha, curv_t - matmul(square, alpha, 1, 0, HIGHEST), 0, 0, HIGHEST)
    )
    beta = matmul(norm_inverse, norm_next, 1, 0, HIGHEST)
    ahead_mix = unit + beta

    def mix(values, coef):
        return [matmul(coef, values[v], 0, 0, HIGHEST) for v in range(vb)]

    image_alpha = mix(image, alpha)
    field_alpha = mix(field, alpha)
    field_ahead = mix(field, ahead_mix)
    image_ahead = mix(image, ahead_mix)
    direction = [field_ahead[v] - image_alpha[v] for v in range(vb)]
    second_alpha = mix(second, alpha)
    image_next = [image_ahead[v] - second_alpha[v] for v in range(vb)]
    direction_image = matmul(ahead_mix, curv, 0, 0, HIGHEST) - matmul(
        alpha, square, 0, 0, HIGHEST
    )
    image_direction = matmul(curv_t, ahead_mix, 1, 0, HIGHEST) - matmul(
        square, alpha, 1, 0, HIGHEST
    )
    known = matmul(direction_image, ahead_mix, 1, 0, HIGHEST)
    known_t = matmul(ahead_mix, image_direction, 0, 0, HIGHEST)
    weights = jnp.concatenate([ahead_mix, -alpha], axis=0)
    packed = gathered(1)
    tall = jnp.concatenate(
        [packed[:, width * g : width * (g + 1)] for g in range(groups)], axis=0
    )
    wide = jnp.concatenate(
        [
            packed[:, groups * width + 2 * width * g : groups * width + 2 * width * (g + 1)]
            for g in range(groups // 2)
        ],
        axis=0,
    )
    last = known - matmul(matmul(weights, tall, 0, 0, HIGHEST), alpha, 1, 0, HIGHEST)
    last_t = known_t - matmul(alpha, matmul(wide, weights, 1, 0, HIGHEST), 0, 0, HIGHEST)
    (alpha_next,) = eliminate([(0.5 * (last + last_t), norm_next)])
    direction_alpha = mix(direction, alpha_next)
    image_next_alpha = mix(image_next, alpha_next)
    for v in range(vb):
        solution_ref[v] = field_alpha[v] + direction_alpha[v]
        residual_ref[v] = (field[v] - image_alpha[v]) - image_next_alpha[v]

    finish()


def shards(probes, mass, blocks, slot_rows, slot_cols, slot_count):
    vb, width, nodes = probes.shape
    n_col = lax.axis_size("col")
    n_row = lax.axis_size("row")
    slots = blocks.shape[2]
    nbr = vb * n_col
    total_blocks = vb * n_col * n_row
    plane = total_blocks // 8
    offsets = [0, 1, 2, plane - 1, plane, plane + 1, 2 * plane]
    deltas = sorted(set([o // vb for o in offsets] + [(o + vb - 1) // vb for o in offsets]))
    dists = sorted(
        set(
            (first + d) // n_col
            for first in range(n_col)
            for d in deltas
            if (first + d) // n_col < n_row
        )
    )
    peers = n_row * n_col - 1
    low = jnp.bfloat16
    f32 = jnp.float32

    def twice(shape, dtype):
        return [pltpu.VMEM(shape, dtype), pltpu.VMEM(shape, dtype)]

    links = len(dists) - 1 + n_col - 1
    smem = pl.BlockSpec(memory_space=pltpu.SMEM)
    hbm = pl.BlockSpec(memory_space=pl.ANY)
    vmem = pl.BlockSpec(memory_space=pltpu.VMEM)
    out = jax.ShapeDtypeStruct((vb, width, nodes), f32)
    return pl.pallas_call(
        functools.partial(kernel, n_row, n_col, dists),
        out_shape=(out, out),
        in_specs=[hbm, hbm, hbm, smem, smem, smem],
        out_specs=(vmem, vmem),
        scratch_shapes=[
            pltpu.VMEM((vb, width, nodes), f32),
            pltpu.VMEM((vb, nodes), f32),
            pltpu.VMEM((slots, nodes, nodes), low),
            twice((nbr, 2 * width, nodes), low),
            twice((len(dists) * vb, 2 * width, nodes), low),
            pltpu.VMEM((slots, width, nodes), f32),
            pltpu.VMEM((nbr, width, nodes), f32),
            twice((nbr, width, nodes), SEND),
            twice((len(dists) - 1, vb, width, nodes), SEND),
            twice((n_col - 1, vb, width, nodes), SEND),
            twice((len(dists) - 1, vb, width, nodes), SEND),
            pltpu.VMEM((vb, width, nodes), f32),
            twice((8, 4 * width * width // 8), f32),
            twice((peers, 8, 4 * width * width // 8), f32),
            pltpu.SemaphoreType.DMA((2 + slots,)),
            pltpu.SemaphoreType.DMA((2, links)),
            pltpu.SemaphoreType.DMA((2, links)),
            pltpu.SemaphoreType.DMA((2, links)),
            pltpu.SemaphoreType.DMA((2, links)),
            pltpu.SemaphoreType.DMA((2, peers)),
            pltpu.SemaphoreType.DMA((2, peers)),
        ],
        compiler_params=pltpu.CompilerParams(
            collective_id=0, has_side_effects=True, vmem_limit_bytes=57 * 1024 * 1024
        ),
    )(probes, mass, blocks, slot_rows, slot_cols, slot_count)


def solution(mesh):
    placed = (
        P(("grp", "row", "col"), None, None),
        P(("grp", "row", "col"), None),
        P(("grp", "row"), "col", None, None, None),
        P(("grp", "row"), "col", None),
        P(("grp", "row"), "col", None),
        P(("grp", "row"), "col"),
    )
    return jax.shard_map(
        shards,
        mesh=mesh,
        in_specs=placed,
        out_specs=(P(("grp", "row", "col"), None, None), P(("grp", "row", "col"), None, None)),
        check_vma=False,
    )
```

```python
import functools
import jax
import jax.numpy as jnp
from jax import lax
from jax.experimental import pallas as pl
from jax.experimental.pallas import tpu as pltpu
from jax.sharding import PartitionSpec as P

MESH = pl.DeviceIdType.MESH
HIGHEST = lax.Precision.HIGHEST
SEND = jnp.bfloat16


def matmul(a, b, a_dim, b_dim, precision=None):
    return lax.dot_general(
        a,
        b,
        (((a_dim,), (b_dim,)), ((), ())),
        precision=precision,
        preferred_element_type=jnp.float32,
    )


def repeat(count, body):
    if count <= 16:
        for k in range(count):
            body(k)
    else:
        lax.fori_loop(0, count, lambda k, c: (body(k), c)[1], 0)


def eliminate(systems):
    size = systems[0][0].shape[0]
    rows = lax.broadcasted_iota(jnp.int32, (size, 1), 0)
    for k in range(size):
        after = []
        for left, right in systems:
            left_k = left[k : k + 1, :]
            right_k = right[k : k + 1, :]
            inverse = 1.0 / left[k : k + 1, k : k + 1]
            left_k = left_k * inverse
            right_k = right_k * inverse
            factor = left[:, k : k + 1]
            here = rows == k
            after.append(
                (
                    jnp.where(here, left_k, left - factor * left_k),
                    jnp.where(here, right_k, right - factor * right_k),
                )
            )
        systems = after
    return [right for _, right in systems]


def kernel(
    n_row,
    n_col,
    dists,
    probes_hbm,
    mass_hbm,
    blocks_hbm,
    rows_ref,
    cols_ref,
    count_ref,
    result_ref,
    field,
    mass,
    tiles,
    row_field,
    col_field,
    products,
    row_sum,
    row_send,
    col_send,
    row_recv,
    col_recv,
    image,
    gram_send,
    gram_recv,
    in_sem,
    a_send_sem,
    a_recv_sem,
    b_send_sem,
    b_recv_sem,
    g_send_sem,
    g_recv_sem,
):
    row_at = lax.axis_index("row")
    col_at = lax.axis_index("col")
    vb, width, nodes = field.shape
    slots = tiles.shape[0]
    nbr = vb * n_col
    peers = n_row * n_col - 1
    me = row_at * n_col + col_at

    def peer_of(k):
        at = lax.rem(me + k + 1, n_row * n_col)
        return {"row": at // n_col, "col": lax.rem(at, n_col)}

    def col_peer(k):
        return lax.rem(col_at + k, n_col)

    def row_peer(d):
        return lax.rem(row_at + d, n_row)

    loads = [
        pltpu.make_async_copy(probes_hbm, field, in_sem.at[0]),
        pltpu.make_async_copy(mass_hbm, mass, in_sem.at[1]),
    ]
    for s in range(slots):
        loads.append(pltpu.make_async_copy(blocks_hbm.at[0, 0, s], tiles.at[s], in_sem.at[2 + s]))
    for load in loads:
        load.start()

    barrier = pltpu.get_barrier_semaphore()

    near = [{"row": row_peer(k), "col": col_at} for k in range(1, n_row)]
    near += [{"row": row_at, "col": col_peer(k)} for k in range(1, n_col)]
    for peer in near:
        pl.semaphore_signal(barrier, inc=1, device_id=peer, device_id_type=MESH)

    live_count = count_ref[0, 0]
    limits, row_of, col_of, row_at_index, col_at_index = [], [], [], [], []
    for s in range(slots):
        live = s < live_count
        lrow = jnp.where(live, rows_ref[0, 0, s], 0)
        lcol = jnp.where(live, cols_ref[0, 0, s], row_at * vb)
        dist = lcol // vb - row_at
        place = jnp.int32(0)
        for at, d in enumerate(dists):
            place = place + jnp.where(dist == d, at, 0)
        part = lax.rem(lcol, vb)
        grow = row_at * nbr + lrow
        gcol = (lcol // vb * n_col + col_at) * vb + part
        limits.append(jnp.where(live, jnp.where(grow == gcol, 0, -nodes), nodes))
        row_of.append(lrow)
        col_of.append(place * vb + part)
        col_at_index.append(place * vb + part)
        row_at_index.append(
            lax.rem(col_at - lrow // vb + n_col, n_col) * vb + lax.rem(lrow, vb)
        )

    def field_to_rows(step):
        to_rows = {}
        for at in range(1, len(dists)):
            to_rows["fr", step, at] = pltpu.make_async_remote_copy(
                src_ref=col_field[step].at[pl.ds(0, vb)],
                dst_ref=col_field[step].at[pl.ds(at * vb, vb)],
                send_sem=a_send_sem.at[step, at - 1],
                recv_sem=a_recv_sem.at[step, at - 1],
                device_id={"row": row_peer(n_row - dists[at]), "col": col_at},
                device_id_type=MESH,
            )
        return to_rows

    def field_to_cols(step):
        to_cols = {}
        for k in range(1, n_col):
            sem = len(dists) - 2 + k
            to_cols["fc", step, k] = pltpu.make_async_remote_copy(
                src_ref=row_field[step].at[pl.ds(0, vb)],
                dst_ref=row_field[step].at[pl.ds(k * vb, vb)],
                send_sem=a_send_sem.at[step, sem],
                recv_sem=a_recv_sem.at[step, sem],
                device_id={"row": row_at, "col": col_peer(k)},
                device_id_type=MESH,
            )
        return to_cols

    def parts_to_cols(step):
        to_cols = {}
        for k in range(1, n_col):
            to_cols["pc", step, k] = pltpu.make_async_remote_copy(
                src_ref=row_send[step].at[pl.ds(col_peer(k) * vb, vb)],
                dst_ref=row_recv[step].at[k - 1],
                send_sem=b_send_sem.at[step, k - 1],
                recv_sem=b_recv_sem.at[step, k - 1],
                device_id={"row": row_at, "col": col_peer(k)},
                device_id_type=MESH,
            )
        return to_cols

    def parts_to_rows(step):
        to_rows = {}
        for at in range(1, len(dists)):
            sem = n_col - 2 + at
            to_rows["pr", step, at] = pltpu.make_async_remote_copy(
                src_ref=col_send[step].at[at - 1],
                dst_ref=col_recv[step].at[at - 1],
                send_sem=b_send_sem.at[step, sem],
                recv_sem=b_recv_sem.at[step, sem],
                device_id={"row": row_peer(dists[at]), "col": col_at},
                device_id_type=MESH,
            )
        return to_rows

    def gram_copy(step, k):
        return pltpu.make_async_remote_copy(
            src_ref=gram_send[step],
            dst_ref=gram_recv[step].at[k],
            send_sem=g_send_sem.at[step, k],
            recv_sem=g_recv_sem.at[step, k],
            device_id=peer_of(k),
            device_id_type=MESH,
        )

    def publish(step, values):
        for v in range(vb):
            high = values[v].astype(jnp.bfloat16)
            low = (values[v] - high.astype(jnp.float32)).astype(jnp.bfloat16)
            for ref in (row_field[step], col_field[step]):
                ref[v, 0:width] = high
                ref[v, width : 2 * width] = low

    def product(values, tile, dim):
        both = matmul(values, tile, 1, dim)
        return both[0:width] + both[width : 2 * width]

    sent, arrived = {}, set()

    def start(copies):
        for key, copy in copies.items():
            copy.start()
            sent[key] = copy

    def arrive(copies):
        for key, copy in copies.items():
            copy.wait_recv()
            arrived.add(key)

    grams_sent, grams_in = [], []

    def start_grams(step):
        repeat(peers, lambda k: gram_copy(step, k).start())
        grams_sent.append(step)

    def scattered(targets, of):
        sums = []
        for target in range(targets):
            total = jnp.zeros((width, nodes), jnp.float32)
            for s in range(slots):
                total = total + jnp.where(of[s] == target, products[s], 0.0)
            sums.append(total)
        return sums

    def forward(step):
        arrive(field_to_rows(step))
        for s in range(slots):
            products[s] = product(col_field[step][col_at_index[s]], tiles[s], 1)
        for target, total in enumerate(scattered(nbr, row_of)):
            row_sum[target] = total
            row_send[step][target] = total.astype(SEND)
        start(parts_to_cols(step))

    def backward(step):
        arrive(field_to_cols(step))
        for s in range(slots):
            products[s] = product(row_field[step][row_at_index[s]], tiles[s], 0)
        sums = scattered(len(dists) * vb, col_of)
        for at in range(1, len(dists)):
            for v in range(vb):
                col_send[step][at - 1, v] = sums[at * vb + v].astype(SEND)
        start(parts_to_rows(step))
        return [sums[v] + row_sum[col_at * vb + v] for v in range(vb)]

    def combined(step, totals):
        arrive(parts_to_cols(step) | parts_to_rows(step))
        for k in range(n_col - 1):
            totals = [totals[v] + row_recv[step][k, v].astype(jnp.float32) for v in range(vb)]
        for at in range(len(dists) - 1):
            totals = [totals[v] + col_recv[step][at, v].astype(jnp.float32) for v in range(vb)]
        return totals

    def finish():
        for copy in sent.values():
            copy.wait_send()
        for step in grams_sent:
            repeat(peers, lambda k: gram_copy(step, k).wait_send())

    loads[0].wait()
    publish(0, field)
    pl.semaphore_wait(barrier, len(near))
    start(field_to_rows(0) | field_to_cols(0))
    ahead = lax.broadcasted_iota(jnp.int32, (nodes, nodes), 1) - lax.broadcasted_iota(
        jnp.int32, (nodes, nodes), 0
    )
    loads[1].wait()
    for s in range(slots):
        loads[2 + s].wait()
        tiles[s] = jnp.where(ahead > limits[s], tiles[s], jnp.zeros_like(tiles[s]))
    forward(0)
    totals = combined(0, backward(0))
    for v in range(vb):
        image[v] = totals[v] + mass[v : v + 1, :] * field[v]

    publish(1, image)
    start(field_to_rows(1) | field_to_cols(1))

    def gram(first, second):
        total = None
        for v in range(vb):
            both = jnp.concatenate([first[v], second[v]], axis=0)
            term = matmul(both, both, 1, 1, HIGHEST)
            total = term if total is None else total + term
        return total

    groups = 2 * width // 8

    def pack(step, total):
        for g in range(groups):
            gram_send[step][:, 2 * width * g : 2 * width * (g + 1)] = total[8 * g : 8 * (g + 1)]

    def unpack(packed):
        total = jnp.concatenate(
            [packed[:, 2 * width * g : 2 * width * (g + 1)] for g in range(groups)], axis=0
        )
        upper, lower = total[0:width], total[width : 2 * width]
        return upper[:, 0:width], upper[:, width:], lower[:, 0:width], lower[:, width:]

    pack(0, gram(field, image))
    forward(1)
    start_grams(0)
    totals = backward(1)
    totals = combined(1, totals)
    second = [totals[v] + mass[v : v + 1, :] * image[v] for v in range(vb)]
    tall, wide = None, None
    for v in range(vb):
        both = jnp.concatenate([field[v], image[v]], axis=0)
        down = matmul(both, second[v], 1, 1, HIGHEST)
        across = matmul(second[v], both, 1, 1, HIGHEST)
        tall = down if tall is None else tall + down
        wide = across if wide is None else wide + across
    for g in range(groups):
        gram_send[1][:, width * g : width * (g + 1)] = tall[8 * g : 8 * (g + 1)]
    for g in range(groups // 2):
        at = groups * width + 2 * width * g
        gram_send[1][:, at : at + 2 * width] = wide[8 * g : 8 * (g + 1)]
    start_grams(1)

    def gathered(step):
        grams_in.append(step)
        repeat(peers, lambda k: gram_copy(step, k).wait_recv())
        total = gram_send[step][...]
        if peers <= 16:
            for k in range(peers):
                total = total + gram_recv[step][k]
            return total
        return lax.fori_loop(0, peers, lambda k, t: t + gram_recv[step][k], total)

    grams = gathered(0)
    norm, curv, curv_t, square = unpack(grams)
    unit = (
        lax.broadcasted_iota(jnp.int32, (width, width), 0)
        == lax.broadcasted_iota(jnp.int32, (width, width), 1)
    ).astype(jnp.float32)
    alpha, norm_inverse = eliminate([(0.5 * (curv + curv_t), norm), (norm, unit)])
    norm_next = (
        norm
        - matmul(curv, alpha, 1, 0, HIGHEST)
        - matmul(alpha, curv_t - matmul(square, alpha, 1, 0, HIGHEST), 0, 0, HIGHEST)
    )
    beta = matmul(norm_inverse, norm_next, 1, 0, HIGHEST)
    ahead_mix = unit + beta

    def mix(values, coef):
        return [matmul(coef, values[v], 0, 0, HIGHEST) for v in range(vb)]

    image_alpha = mix(image, alpha)
    field_alpha = mix(field, alpha)
    field_ahead = mix(field, ahead_mix)
    image_ahead = mix(image, ahead_mix)
    direction = [field_ahead[v] - image_alpha[v] for v in range(vb)]
    second_alpha = mix(second, alpha)
    image_next = [image_ahead[v] - second_alpha[v] for v in range(vb)]
    direction_image = matmul(ahead_mix, curv, 0, 0, HIGHEST) - matmul(
        alpha, square, 0, 0, HIGHEST
    )
    image_direction = matmul(curv_t, ahead_mix, 1, 0, HIGHEST) - matmul(
        square, alpha, 1, 0, HIGHEST
    )
    known = matmul(direction_image, ahead_mix, 1, 0, HIGHEST)
    known_t = matmul(ahead_mix, image_direction, 0, 0, HIGHEST)
    weights = jnp.concatenate([ahead_mix, -alpha], axis=0)
    packed = gathered(1)
    tall = jnp.concatenate(
        [packed[:, width * g : width * (g + 1)] for g in range(groups)], axis=0
    )
    wide = jnp.concatenate(
        [
            packed[:, groups * width + 2 * width * g : groups * width + 2 * width * (g + 1)]
            for g in range(groups // 2)
        ],
        axis=0,
    )
    last = known - matmul(matmul(weights, tall, 0, 0, HIGHEST), alpha, 1, 0, HIGHEST)
    last_t = known_t - matmul(alpha, matmul(wide, weights, 1, 0, HIGHEST), 0, 0, HIGHEST)
    (alpha_next,) = eliminate([(0.5 * (last + last_t), norm_next)])
    direction_alpha = mix(direction, alpha_next)
    image_next_alpha = mix(image_next, alpha_next)
    for v in range(vb):
        result_ref[0, v] = field_alpha[v] + direction_alpha[v]
        result_ref[1, v] = (field[v] - image_alpha[v]) - image_next_alpha[v]

    finish()


def shards(probes, mass, blocks, slot_rows, slot_cols, slot_count):
    vb, width, nodes = probes.shape
    n_col = lax.axis_size("col")
    n_row = lax.axis_size("row")
    slots = blocks.shape[2]
    nbr = vb * n_col
    total_blocks = vb * n_col * n_row
    plane = total_blocks // 8
    offsets = [0, 1, 2, plane - 1, plane, plane + 1, 2 * plane]
    deltas = sorted(set([o // vb for o in offsets] + [(o + vb - 1) // vb for o in offsets]))
    dists = sorted(
        set(
            (first + d) // n_col
            for first in range(n_col)
            for d in deltas
            if (first + d) // n_col < n_row
        )
    )
    peers = n_row * n_col - 1
    low = jnp.bfloat16
    f32 = jnp.float32

    def twice(shape, dtype):
        return [pltpu.VMEM(shape, dtype), pltpu.VMEM(shape, dtype)]

    links = len(dists) - 1 + n_col - 1
    smem = pl.BlockSpec(memory_space=pltpu.SMEM)
    hbm = pl.BlockSpec(memory_space=pl.ANY)
    vmem = pl.BlockSpec(memory_space=pltpu.VMEM)
    out = jax.ShapeDtypeStruct((vb, width, nodes), f32)
    both = pl.pallas_call(
        functools.partial(kernel, n_row, n_col, dists),
        out_shape=jax.ShapeDtypeStruct((2, vb, width, nodes), f32),
        in_specs=[hbm, hbm, hbm, smem, smem, smem],
        out_specs=vmem,
        scratch_shapes=[
            pltpu.VMEM((vb, width, nodes), f32),
            pltpu.VMEM((vb, nodes), f32),
            pltpu.VMEM((slots, nodes, nodes), low),
            twice((nbr, 2 * width, nodes), low),
            twice((len(dists) * vb, 2 * width, nodes), low),
            pltpu.VMEM((slots, width, nodes), f32),
            pltpu.VMEM((nbr, width, nodes), f32),
            twice((nbr, width, nodes), SEND),
            twice((len(dists) - 1, vb, width, nodes), SEND),
            twice((n_col - 1, vb, width, nodes), SEND),
            twice((len(dists) - 1, vb, width, nodes), SEND),
            pltpu.VMEM((vb, width, nodes), f32),
            twice((8, 4 * width * width // 8), f32),
            twice((peers, 8, 4 * width * width // 8), f32),
            pltpu.SemaphoreType.DMA((2 + slots,)),
            pltpu.SemaphoreType.DMA((2, links)),
            pltpu.SemaphoreType.DMA((2, links)),
            pltpu.SemaphoreType.DMA((2, links)),
            pltpu.SemaphoreType.DMA((2, links)),
            pltpu.SemaphoreType.DMA((2, peers)),
            pltpu.SemaphoreType.DMA((2, peers)),
        ],
        compiler_params=pltpu.CompilerParams(
            collective_id=0, has_side_effects=True, vmem_limit_bytes=57 * 1024 * 1024
        ),
    )(probes, mass, blocks, slot_rows, slot_cols, slot_count)
    return both[0], both[1]


def solution(mesh):
    placed = (
        P(("grp", "row", "col"), None, None),
        P(("grp", "row", "col"), None),
        P(("grp", "row"), "col", None, None, None),
        P(("grp", "row"), "col", None),
        P(("grp", "row"), "col", None),
        P(("grp", "row"), "col"),
    )
    return jax.shard_map(
        shards,
        mesh=mesh,
        in_specs=placed,
        out_specs=(P(("grp", "row", "col"), None, None), P(("grp", "row", "col"), None, None)),
        check_vma=False,
    )
```

```python
import functools
import jax
import jax.numpy as jnp
from jax import lax
from jax.experimental import pallas as pl
from jax.experimental.pallas import tpu as pltpu
from jax.sharding import PartitionSpec as P

MESH = pl.DeviceIdType.MESH
HIGHEST = lax.Precision.HIGHEST
SEND = jnp.bfloat16


def matmul(a, b, a_dim, b_dim, precision=None):
    return lax.dot_general(
        a,
        b,
        (((a_dim,), (b_dim,)), ((), ())),
        precision=precision,
        preferred_element_type=jnp.float32,
    )


def repeat(count, body):
    if count <= 16:
        for k in range(count):
            body(k)
    else:
        lax.fori_loop(0, count, lambda k, c: (body(k), c)[1], 0)


def eliminate(systems):
    size = systems[0][0].shape[0]
    rows = lax.broadcasted_iota(jnp.int32, (size, 1), 0)
    for k in range(size):
        after = []
        for left, right in systems:
            left_k = left[k : k + 1, :]
            right_k = right[k : k + 1, :]
            inverse = 1.0 / left[k : k + 1, k : k + 1]
            left_k = left_k * inverse
            right_k = right_k * inverse
            factor = left[:, k : k + 1]
            here = rows == k
            after.append(
                (
                    jnp.where(here, left_k, left - factor * left_k),
                    jnp.where(here, right_k, right - factor * right_k),
                )
            )
        systems = after
    return [right for _, right in systems]


def kernel(
    n_row,
    n_col,
    dists,
    probes_hbm,
    mass_hbm,
    blocks_hbm,
    rows_ref,
    cols_ref,
    count_ref,
    result_ref,
    field,
    mass,
    tiles,
    row_field,
    col_field,
    products,
    row_sum,
    row_send,
    col_send,
    row_recv,
    col_recv,
    image,
    gram_send,
    gram_recv,
    in_sem,
    a_send_sem,
    a_recv_sem,
    b_send_sem,
    b_recv_sem,
    g_send_sem,
    g_recv_sem,
):
    row_at = lax.axis_index("row")
    col_at = lax.axis_index("col")
    vb, width, nodes = field.shape
    slots = tiles.shape[0]
    nbr = vb * n_col
    peers = n_row * n_col - 1
    me = row_at * n_col + col_at

    def peer_of(k):
        at = lax.rem(me + k + 1, n_row * n_col)
        return {"row": at // n_col, "col": lax.rem(at, n_col)}

    def col_peer(k):
        return lax.rem(col_at + k, n_col)

    def row_peer(d):
        return lax.rem(row_at + d, n_row)

    loads = [
        pltpu.make_async_copy(probes_hbm, field, in_sem.at[0]),
        pltpu.make_async_copy(mass_hbm, mass, in_sem.at[1]),
    ]
    for s in range(slots):
        loads.append(pltpu.make_async_copy(blocks_hbm.at[0, 0, s], tiles.at[s], in_sem.at[2 + s]))
    for load in loads:
        load.start()

    barrier = pltpu.get_barrier_semaphore()

    near = [{"row": row_peer(k), "col": col_at} for k in range(1, n_row)]
    near += [{"row": row_at, "col": col_peer(k)} for k in range(1, n_col)]
    for peer in near:
        pl.semaphore_signal(barrier, inc=1, device_id=peer, device_id_type=MESH)

    live_count = count_ref[0, 0]
    limits, row_of, col_of, row_at_index, col_at_index = [], [], [], [], []
    for s in range(slots):
        live = s < live_count
        lrow = jnp.where(live, rows_ref[0, 0, s], 0)
        lcol = jnp.where(live, cols_ref[0, 0, s], row_at * vb)
        dist = lcol // vb - row_at
        place = jnp.int32(0)
        for at, d in enumerate(dists):
            place = place + jnp.where(dist == d, at, 0)
        part = lax.rem(lcol, vb)
        grow = row_at * nbr + lrow
        gcol = (lcol // vb * n_col + col_at) * vb + part
        limits.append(jnp.where(live, jnp.where(grow == gcol, 0, -nodes), nodes))
        row_of.append(lrow)
        col_of.append(place * vb + part)
        col_at_index.append(place * vb + part)
        row_at_index.append(
            lax.rem(col_at - lrow // vb + n_col, n_col) * vb + lax.rem(lrow, vb)
        )

    def field_to_rows(step):
        to_rows = {}
        for at in range(1, len(dists)):
            to_rows["fr", step, at] = pltpu.make_async_remote_copy(
                src_ref=col_field[step].at[pl.ds(0, vb)],
                dst_ref=col_field[step].at[pl.ds(at * vb, vb)],
                send_sem=a_send_sem.at[step, at - 1],
                recv_sem=a_recv_sem.at[step, at - 1],
                device_id={"row": row_peer(n_row - dists[at]), "col": col_at},
                device_id_type=MESH,
            )
        return to_rows

    def field_to_cols(step):
        to_cols = {}
        for k in range(1, n_col):
            sem = len(dists) - 2 + k
            to_cols["fc", step, k] = pltpu.make_async_remote_copy(
                src_ref=row_field[step].at[pl.ds(0, vb)],
                dst_ref=row_field[step].at[pl.ds(k * vb, vb)],
                send_sem=a_send_sem.at[step, sem],
                recv_sem=a_recv_sem.at[step, sem],
                device_id={"row": row_at, "col": col_peer(k)},
                device_id_type=MESH,
            )
        return to_cols

    def parts_to_cols(step):
        to_cols = {}
        for k in range(1, n_col):
            to_cols["pc", step, k] = pltpu.make_async_remote_copy(
                src_ref=row_send[step].at[pl.ds(col_peer(k) * vb, vb)],
                dst_ref=row_recv[step].at[k - 1],
                send_sem=b_send_sem.at[step, k - 1],
                recv_sem=b_recv_sem.at[step, k - 1],
                device_id={"row": row_at, "col": col_peer(k)},
                device_id_type=MESH,
            )
        return to_cols

    def parts_to_rows(step):
        to_rows = {}
        for at in range(1, len(dists)):
            sem = n_col - 2 + at
            to_rows["pr", step, at] = pltpu.make_async_remote_copy(
                src_ref=col_send[step].at[at - 1],
                dst_ref=col_recv[step].at[at - 1],
                send_sem=b_send_sem.at[step, sem],
                recv_sem=b_recv_sem.at[step, sem],
                device_id={"row": row_peer(dists[at]), "col": col_at},
                device_id_type=MESH,
            )
        return to_rows

    def gram_copy(step, k):
        return pltpu.make_async_remote_copy(
            src_ref=gram_send[step],
            dst_ref=gram_recv[step].at[k],
            send_sem=g_send_sem.at[step, k],
            recv_sem=g_recv_sem.at[step, k],
            device_id=peer_of(k),
            device_id_type=MESH,
        )

    def publish(step, values):
        for v in range(vb):
            high = values[v].astype(jnp.bfloat16)
            low = (values[v] - high.astype(jnp.float32)).astype(jnp.bfloat16)
            for ref in (row_field[step], col_field[step]):
                ref[v, 0:width] = high
                ref[v, width : 2 * width] = low

    def product(values, tile, dim):
        both = matmul(values, tile, 1, dim)
        return both[0:width] + both[width : 2 * width]

    sent, arrived = {}, set()

    def start(copies):
        for key, copy in copies.items():
            copy.start()
            sent[key] = copy

    def arrive(copies):
        for key, copy in copies.items():
            copy.wait_recv()
            arrived.add(key)

    grams_sent, grams_in = [], []

    def start_grams(step):
        repeat(peers, lambda k: gram_copy(step, k).start())
        grams_sent.append(step)

    def scattered(targets, of):
        sums = []
        for target in range(targets):
            total = jnp.zeros((width, nodes), jnp.float32)
            for s in range(slots):
                total = total + jnp.where(of[s] == target, products[s], 0.0)
            sums.append(total)
        return sums

    def forward(step):
        arrive(field_to_rows(step))
        for s in range(slots):
            products[s] = product(col_field[step][col_at_index[s]], tiles[s], 1)
        for target, total in enumerate(scattered(nbr, row_of)):
            row_sum[target] = total
            row_send[step][target] = total.astype(SEND)
        start(parts_to_cols(step))

    def backward(step):
        arrive(field_to_cols(step))
        for s in range(slots):
            products[s] = product(row_field[step][row_at_index[s]], tiles[s], 0)
        sums = scattered(len(dists) * vb, col_of)
        for at in range(1, len(dists)):
            for v in range(vb):
                col_send[step][at - 1, v] = sums[at * vb + v].astype(SEND)
        start(parts_to_rows(step))
        return [sums[v] + row_sum[col_at * vb + v] for v in range(vb)]

    def combined(step, totals):
        arrive(parts_to_cols(step) | parts_to_rows(step))
        for k in range(n_col - 1):
            totals = [totals[v] + row_recv[step][k, v].astype(jnp.float32) for v in range(vb)]
        for at in range(len(dists) - 1):
            totals = [totals[v] + col_recv[step][at, v].astype(jnp.float32) for v in range(vb)]
        return totals

    def finish():
        for copy in sent.values():
            copy.wait_send()
        for step in grams_sent:
            repeat(peers, lambda k: gram_copy(step, k).wait_send())

    loads[0].wait()
    publish(0, field)
    pl.semaphore_wait(barrier, len(near))
    start(field_to_rows(0) | field_to_cols(0))
    ahead = lax.broadcasted_iota(jnp.int32, (nodes, nodes), 1) - lax.broadcasted_iota(
        jnp.int32, (nodes, nodes), 0
    )
    loads[1].wait()
    for s in range(slots):
        loads[2 + s].wait()
        tiles[s] = jnp.where(ahead > limits[s], tiles[s], jnp.zeros_like(tiles[s]))
    forward(0)
    totals = combined(0, backward(0))
    for v in range(vb):
        image[v] = totals[v] + mass[v : v + 1, :] * field[v]

    publish(1, image)
    start(field_to_rows(1) | field_to_cols(1))

    def gram(first, second):
        total = None
        for v in range(vb):
            both = jnp.concatenate([first[v], second[v]], axis=0)
            term = matmul(both, both, 1, 1, HIGHEST)
            total = term if total is None else total + term
        return total

    groups = 2 * width // 8

    def pack(step, total):
        for g in range(groups):
            gram_send[step][:, 2 * width * g : 2 * width * (g + 1)] = total[8 * g : 8 * (g + 1)]

    def unpack(packed):
        total = jnp.concatenate(
            [packed[:, 2 * width * g : 2 * width * (g + 1)] for g in range(groups)], axis=0
        )
        upper, lower = total[0:width], total[width : 2 * width]
        return upper[:, 0:width], upper[:, width:], lower[:, 0:width], lower[:, width:]

    pack(0, gram(field, image))
    forward(1)
    start_grams(0)
    totals = backward(1)
    totals = combined(1, totals)
    second = [totals[v] + mass[v : v + 1, :] * image[v] for v in range(vb)]
    tall, wide = None, None
    for v in range(vb):
        both = jnp.concatenate([field[v], image[v]], axis=0)
        down = matmul(both, second[v], 1, 1, HIGHEST)
        across = matmul(second[v], both, 1, 1, HIGHEST)
        tall = down if tall is None else tall + down
        wide = across if wide is None else wide + across
    for g in range(groups):
        gram_send[1][:, width * g : width * (g + 1)] = tall[8 * g : 8 * (g + 1)]
    for g in range(groups // 2):
        at = groups * width + 2 * width * g
        gram_send[1][:, at : at + 2 * width] = wide[8 * g : 8 * (g + 1)]
    start_grams(1)

    def gathered(step):
        grams_in.append(step)
        repeat(peers, lambda k: gram_copy(step, k).wait_recv())
        total = gram_send[step][...]
        if peers <= 16:
            for k in range(peers):
                total = total + gram_recv[step][k]
            return total
        return lax.fori_loop(0, peers, lambda k, t: t + gram_recv[step][k], total)

    grams = gathered(0)
    norm, curv, curv_t, square = unpack(grams)
    unit = (
        lax.broadcasted_iota(jnp.int32, (width, width), 0)
        == lax.broadcasted_iota(jnp.int32, (width, width), 1)
    ).astype(jnp.float32)
    alpha, norm_inverse = eliminate([(0.5 * (curv + curv_t), norm), (norm, unit)])
    norm_next = (
        norm
        - matmul(curv, alpha, 1, 0, HIGHEST)
        - matmul(alpha, curv_t - matmul(square, alpha, 1, 0, HIGHEST), 0, 0, HIGHEST)
    )
    beta = matmul(norm_inverse, norm_next, 1, 0, HIGHEST)
    ahead_mix = unit + beta

    def mix(values, coef):
        return [matmul(coef, values[v], 0, 0, HIGHEST) for v in range(vb)]

    image_alpha = mix(image, alpha)
    field_alpha = mix(field, alpha)
    field_ahead = mix(field, ahead_mix)
    image_ahead = mix(image, ahead_mix)
    direction = [field_ahead[v] - image_alpha[v] for v in range(vb)]
    second_alpha = mix(second, alpha)
    image_next = [image_ahead[v] - second_alpha[v] for v in range(vb)]
    direction_image = matmul(ahead_mix, curv, 0, 0, HIGHEST) - matmul(
        alpha, square, 0, 0, HIGHEST
    )
    image_direction = matmul(curv_t, ahead_mix, 1, 0, HIGHEST) - matmul(
        square, alpha, 1, 0, HIGHEST
    )
    known = matmul(direction_image, ahead_mix, 1, 0, HIGHEST)
    known_t = matmul(ahead_mix, image_direction, 0, 0, HIGHEST)
    weights = jnp.concatenate([ahead_mix, -alpha], axis=0)
    finish()
    packed = gathered(1)
    tall = jnp.concatenate(
        [packed[:, width * g : width * (g + 1)] for g in range(groups)], axis=0
    )
    wide = jnp.concatenate(
        [
            packed[:, groups * width + 2 * width * g : groups * width + 2 * width * (g + 1)]
            for g in range(groups // 2)
        ],
        axis=0,
    )
    last = known - matmul(matmul(weights, tall, 0, 0, HIGHEST), alpha, 1, 0, HIGHEST)
    last_t = known_t - matmul(alpha, matmul(wide, weights, 1, 0, HIGHEST), 0, 0, HIGHEST)
    (alpha_next,) = eliminate([(0.5 * (last + last_t), norm_next)])
    direction_alpha = mix(direction, alpha_next)
    image_next_alpha = mix(image_next, alpha_next)
    for v in range(vb):
        result_ref[0, v] = field_alpha[v] + direction_alpha[v]
        result_ref[1, v] = (field[v] - image_alpha[v]) - image_next_alpha[v]


def shards(probes, mass, blocks, slot_rows, slot_cols, slot_count):
    vb, width, nodes = probes.shape
    n_col = lax.axis_size("col")
    n_row = lax.axis_size("row")
    slots = blocks.shape[2]
    nbr = vb * n_col
    total_blocks = vb * n_col * n_row
    plane = total_blocks // 8
    offsets = [0, 1, 2, plane - 1, plane, plane + 1, 2 * plane]
    deltas = sorted(set([o // vb for o in offsets] + [(o + vb - 1) // vb for o in offsets]))
    dists = sorted(
        set(
            (first + d) // n_col
            for first in range(n_col)
            for d in deltas
            if (first + d) // n_col < n_row
        )
    )
    peers = n_row * n_col - 1
    low = jnp.bfloat16
    f32 = jnp.float32

    def twice(shape, dtype):
        return [pltpu.VMEM(shape, dtype), pltpu.VMEM(shape, dtype)]

    links = len(dists) - 1 + n_col - 1
    smem = pl.BlockSpec(memory_space=pltpu.SMEM)
    hbm = pl.BlockSpec(memory_space=pl.ANY)
    vmem = pl.BlockSpec(memory_space=pltpu.VMEM)
    out = jax.ShapeDtypeStruct((vb, width, nodes), f32)
    both = pl.pallas_call(
        functools.partial(kernel, n_row, n_col, dists),
        out_shape=jax.ShapeDtypeStruct((2, vb, width, nodes), f32),
        in_specs=[hbm, hbm, hbm, smem, smem, smem],
        out_specs=vmem,
        scratch_shapes=[
            pltpu.VMEM((vb, width, nodes), f32),
            pltpu.VMEM((vb, nodes), f32),
            pltpu.VMEM((slots, nodes, nodes), low),
            twice((nbr, 2 * width, nodes), low),
            twice((len(dists) * vb, 2 * width, nodes), low),
            pltpu.VMEM((slots, width, nodes), f32),
            pltpu.VMEM((nbr, width, nodes), f32),
            twice((nbr, width, nodes), SEND),
            twice((len(dists) - 1, vb, width, nodes), SEND),
            twice((n_col - 1, vb, width, nodes), SEND),
            twice((len(dists) - 1, vb, width, nodes), SEND),
            pltpu.VMEM((vb, width, nodes), f32),
            twice((8, 4 * width * width // 8), f32),
            twice((peers, 8, 4 * width * width // 8), f32),
            pltpu.SemaphoreType.DMA((2 + slots,)),
            pltpu.SemaphoreType.DMA((2, links)),
            pltpu.SemaphoreType.DMA((2, links)),
            pltpu.SemaphoreType.DMA((2, links)),
            pltpu.SemaphoreType.DMA((2, links)),
            pltpu.SemaphoreType.DMA((2, peers)),
            pltpu.SemaphoreType.DMA((2, peers)),
        ],
        compiler_params=pltpu.CompilerParams(
            collective_id=0, has_side_effects=True, vmem_limit_bytes=57 * 1024 * 1024
        ),
    )(probes, mass, blocks, slot_rows, slot_cols, slot_count)
    return both[0], both[1]


def solution(mesh):
    placed = (
        P(("grp", "row", "col"), None, None),
        P(("grp", "row", "col"), None),
        P(("grp", "row"), "col", None, None, None),
        P(("grp", "row"), "col", None),
        P(("grp", "row"), "col", None),
        P(("grp", "row"), "col"),
    )
    return jax.shard_map(
        shards,
        mesh=mesh,
        in_specs=placed,
        out_specs=(P(("grp", "row", "col"), None, None), P(("grp", "row", "col"), None, None)),
        check_vma=False,
    )
```
